32 devices in a mesh: ctx: 16 (over z, x, core), tp: 2 (over y).
Axes of the slice: x: 2, y: 2, z: 4, core: 2. Of those that a mesh axis runs over, the one named last changes fastest.
Arguments:
- states: bfloat16 [4096, 1024], P('ctx'), may hold values from -6 to 6
- span_order: int32 [16, 4], P('ctx'), may hold values from 0 to 31, as said below
- attn_gain: bfloat16 [1024], P('ctx'), may hold values from 0.5 to 1.5
- w_query: bfloat16 [1024, 1024], P('ctx', 'tp'), may hold values from -0.1875 to 0.1875
- w_key: bfloat16 [1024, 512], P('ctx', 'tp'), may hold values from -0.1875 to 0.1875
- w_value: bfloat16 [1024, 512], P('ctx', 'tp'), may hold values from -0.1875 to 0.1875
- query_gain: bfloat16 [64], P('ctx'), may hold values from 0.5 to 1.5
- key_gain: bfloat16 [64], P('ctx'), may hold values from 0.5 to 1.5
- w_out: bfloat16 [1024, 1024], P('tp', 'ctx'), may hold values from -1.5 to 1.5
- ffn_gain: bfloat16 [1024], P('ctx'), may hold values from 0.5 to 1.5
- w_gate: bfloat16 [1024, 4608], P('ctx', 'tp'), may hold values from -0.1875 to 0.1875
- w_up: bfloat16 [1024, 4608], P('ctx', 'tp'), may hold values from -0.1875 to 0.1875
- w_down: bfloat16 [4608, 1024], P('tp', 'ctx'), may hold values from -0.09375 to 0.09375
- grad_out: bfloat16 [4096, 1024], P('ctx'), may hold values from -6 to 6
Outputs:
- output: bfloat16 [4096, 1024], P('ctx')
- grad_states: float32 [4096, 1024], P('ctx')
- grad_attn_gain: float32 [1024], P('ctx')
- grad_query: float32 [1024, 1024], P('ctx', 'tp')
- grad_key: float32 [1024, 512], P('ctx', 'tp')
- grad_value: float32 [1024, 512], P('ctx', 'tp')
- grad_query_gain: float32 [64], P('ctx')
- grad_key_gain: float32 [64], P('ctx')
- grad_proj: float32 [1024, 1024], P('tp', 'ctx')
- grad_ffn_gain: float32 [1024], P('ctx')
- grad_gate: float32 [1024, 4608], P('ctx', 'tp')
- grad_up: float32 [1024, 4608], P('ctx', 'tp')
- grad_down: float32 [4608, 1024], P('tp', 'ctx')
The draws below stay inside these ranges and needn't reach their ends.
Inputs may be any that keep to these rules, and one draw needn't show every extreme that they name: `span_order`: in each row c the two columns 2 s and 2 s + 1 hold p and 31 - p for some p; every span of every sequence is held exactly once.
All inputs are finite; a program needn't handle non-finite values.
Results may differ from the reference program's by a relative error of at most 0.03.
Values may be sent and summed in bfloat16 or wider, within the bound.
A program may use at most 128 MiB of HBM per device.

```python
import math
import jax
import jax.numpy as jnp
from jax import lax

D = 1024
H = 16
KV = 8
DH = 64
FF = 4608
SPAN = 64
SEQS = 2
SPANS = 32
TOKENS = 4096


def draw_span_order(key, part):
    key = jax.random.fold_in(key, 7)
    half_count = SPANS // 2
    seq_keys = jax.random.split(key, SEQS)
    lower = jax.vmap(lambda single: jax.random.permutation(single, half_count))(seq_keys)
    lower = jnp.transpose(lower).astype(jnp.int32)
    upper = (SPANS - 1 - lower).astype(jnp.int32)
    return jnp.stack([lower, upper], axis=2).reshape(half_count, 2 * SEQS).astype(jnp.int32)


def level_of(stream_key, extent, cuts, low, high):
    def one(axis_at, parts):
        heights = jax.random.uniform(jax.random.fold_in(jax.random.fold_in(stream_key, 6), axis_at), (parts,), jnp.float32, low / len(cuts), high / len(cuts))
        return jnp.repeat(jnp.exp(heights), extent[axis_at] // parts).reshape((-1,) + (1,) * (len(extent) - axis_at - 1))

    loudness = one(*cuts[0])
    for cut in cuts[1:]:
        loudness = loudness * one(*cut)
    return loudness


def normal_values(rng, dims, deviation, reach, pieces=(), kind=jnp.bfloat16):
    factor_of = level_of(rng, dims, pieces, -0.22, 0.18) if pieces else 1.0
    entries = jax.random.normal(rng, dims, jnp.float32) * deviation * factor_of
    return jnp.minimum(jnp.maximum(entries, -reach), reach).astype(kind)


def setup_inputs(seed: int = 0) -> dict:
    seeds = jax.random.split(jax.random.key(seed), 15)
    states = normal_values(seeds[0], (TOKENS, D), 1.0, 6.0, ((0, 16),))
    span_order = draw_span_order(jax.random.fold_in(seeds[14], 71), 0)
    attn_gain = jnp.clip(1.0 + 0.1 * jax.random.normal(seeds[2], (D,), jnp.float32), 0.5, 1.5).astype(jnp.bfloat16)
    w_query = normal_values(seeds[3], (D, H * DH), D ** -0.5, 0.1875, ((0, 16), (1, 2)))
    w_key = normal_values(seeds[4], (D, KV * DH), D ** -0.5, 0.1875, ((0, 16), (1, 2)))
    w_value = normal_values(seeds[5], (D, KV * DH), D ** -0.5, 0.1875, ((0, 16), (1, 2)))
    query_gain = jnp.clip(1.0 + 0.1 * jax.random.normal(seeds[6], (DH,), jnp.float32), 0.5, 1.5).astype(jnp.bfloat16)
    key_gain = jnp.clip(1.0 + 0.1 * jax.random.normal(seeds[7], (DH,), jnp.float32), 0.5, 1.5).astype(jnp.bfloat16)
    w_out = normal_values(seeds[8], (H * DH, D), (H * DH // 64) ** -0.5, 1.5, ((0, 2), (1, 16)))
    ffn_gain = jnp.clip(1.0 + 0.1 * jax.random.normal(seeds[9], (D,), jnp.float32), 0.5, 1.5).astype(jnp.bfloat16)
    w_gate = normal_values(seeds[10], (D, FF), D ** -0.5, 0.1875, ((0, 16), (1, 2)))
    w_up = normal_values(seeds[11], (D, FF), D ** -0.5, 0.1875, ((0, 16), (1, 2)))
    w_down = normal_values(seeds[12], (FF, D), FF ** -0.5, 0.09375, ((0, 2), (1, 16)))
    grad_out = normal_values(seeds[13], (TOKENS, D), 1.0, 6.0, ((0, 16),))
    return dict(states=states, span_order=span_order, attn_gain=attn_gain, w_query=w_query, w_key=w_key, w_value=w_value, query_gain=query_gain, key_gain=key_gain, w_out=w_out, ffn_gain=ffn_gain, w_gate=w_gate, w_up=w_up, w_down=w_down, grad_out=grad_out)


EPS = 1e-05
THETA = 1000000.0
SCALE = 0.125

@jax.custom_vjp
def low(v):
    return lax.optimization_barrier(v.astype(jnp.bfloat16)).astype(jnp.float32)

@jax.custom_vjp
def low_back(v):
    return v

def low_keep(v):
    return (low(v), None)

def low_pass(kept, grad):
    return (grad,)

def back_keep(v):
    return (v, None)

def back_low(kept, grad):
    return (low(grad),)
low.defvjp(low_keep, low_pass)
low_back.defvjp(back_keep, back_low)

def matmul(left, right):
    return jnp.dot(left, right, precision=lax.Precision.HIGHEST)

def norm_rows(values, gain):
    return values * lax.rsqrt(lax.optimization_barrier(jnp.mean(values * values, axis=-1, keepdims=True)) + EPS) * gain

def rotate(values, cosine, sine_part):
    half_dim = values.shape[-1] // 2
    first_half = values[..., :half_dim]
    second_half = values[..., half_dim:]
    return jnp.concatenate([first_half * cosine - second_half * sine_part, second_half * cosine + first_half * sine_part], axis=-1)

def by_sequence(arranged):
    split = arranged.reshape((SPANS // 2, SEQS, 2 * SPAN) + arranged.shape[1:])
    return jnp.swapaxes(split, 0, 1).reshape((SEQS, SPANS * SPAN) + arranged.shape[1:])

def attend_sequence(query_seq, key_seq, value_seq, place_seq):
    group_size = H // KV
    key_all = jnp.repeat(key_seq, group_size, axis=1)
    value_all = jnp.repeat(value_seq, group_size, axis=1)
    block_rows = math.gcd(query_seq.shape[0], 512)
    block_count = query_seq.shape[0] // block_rows
    query_blocks = query_seq.reshape(block_count, block_rows, H, DH)
    place_blocks = place_seq.reshape(block_count, block_rows)

    def block_step(blocks):
        query_part, place_part = blocks
        scores = jnp.einsum('qhd,khd->hqk', query_part, key_all, precision=lax.Precision.HIGHEST) * SCALE
        scores = low_back(scores)
        visible = place_seq[None, None, :] <= place_part[None, :, None]
        scores = jnp.where(visible, scores, -jnp.inf)
        highest = lax.optimization_barrier(jnp.max(scores, axis=-1, keepdims=True))
        weights = jnp.exp(scores - highest)
        weights = low(weights / lax.optimization_barrier(jnp.sum(weights, axis=-1, keepdims=True)))
        return jnp.einsum('hqk,khd->qhd', weights, value_all, precision=lax.Precision.HIGHEST)
    attended = lax.map(jax.checkpoint(block_step), (query_blocks, place_blocks))
    return attended.reshape(query_seq.shape[0], H, DH)

def forward(states, attn_gain, w_query, w_key, w_value, query_gain, key_gain, w_out, ffn_gain, w_gate, w_up, w_down, place, angles):
    token_rows = states.shape[0]
    cosine = jnp.cos(angles)[:, None, :]
    sine_part = jnp.sin(angles)[:, None, :]
    hidden_one = low(norm_rows(states, attn_gain))
    query_pre = low_back(matmul(hidden_one, w_query)).reshape(token_rows, H, DH)
    key_pre = low_back(matmul(hidden_one, w_key)).reshape(token_rows, KV, DH)
    value_low = low(low_back(matmul(hidden_one, w_value))).reshape(token_rows, KV, DH)
    query_rot = low(rotate(norm_rows(query_pre, query_gain), cosine, sine_part))
    key_rot = low(rotate(norm_rows(key_pre, key_gain), cosine, sine_part))
    attended = lax.map(lambda items: attend_sequence(items[0], items[1], items[2], items[3]), (by_sequence(query_rot), by_sequence(key_rot), by_sequence(value_low), by_sequence(place)))
    attended = jnp.swapaxes(attended.reshape(SEQS, SPANS // 2, 2 * SPAN, H, DH), 0, 1).reshape(token_rows, H * DH)
    mixed = low(low_back(attended))
    middle = states + low_back(matmul(mixed, w_out))
    hidden_two = low(norm_rows(middle, ffn_gain))
    gate_proj = low_back(matmul(hidden_two, w_gate))
    up_proj = low_back(matmul(hidden_two, w_up))
    inner = low(gate_proj / (1.0 + jnp.exp(-gate_proj)) * up_proj)
    return middle + low_back(matmul(inner, w_down))

def reference(states, span_order, attn_gain, w_query, w_key, w_value, query_gain, key_gain, w_out, ffn_gain, w_gate, w_up, w_down, grad_out):
    offsets = jnp.arange(SPAN, dtype=jnp.int32)
    place = (span_order.astype(jnp.int32).reshape(SPANS // 2, SEQS, 2, 1) * SPAN + offsets).reshape(-1).astype(jnp.int32)
    half_dim = DH // 2
    inverse_freq = jnp.exp(-math.log(THETA) * jnp.arange(half_dim, dtype=jnp.float32) / half_dim)
    angles = place.astype(jnp.float32)[:, None] * inverse_freq[None, :]
    floats = [item.astype(jnp.float32) for item in (states, attn_gain, w_query, w_key, w_value, query_gain, key_gain, w_out, ffn_gain, w_gate, w_up, w_down)]

    def whole(*items):
        return forward(*items, place, angles)
    result, pullback = jax.vjp(whole, *floats)
    grads = pullback(grad_out.astype(jnp.float32))
    return (result.astype(jnp.bfloat16), grads[0], grads[1], grads[2], grads[3], grads[4], grads[5], grads[6], grads[7], grads[8], grads[9], grads[10], grads[11])
```

```python
import math

import jax
import jax.numpy as jnp
from jax import lax
from jax.experimental import pallas as pl
from jax.experimental.pallas import tpu as pltpu
from jax.sharding import PartitionSpec as P

DH = 64


EPS = 1e-05
THETA = 1000000.0
SCALE = 0.125


VMEM_LIMIT = 48 * 1024 * 1024
EXTRA_ROWS = 16


def swapped(shard, axis, bit):
    devices = lax.axis_size(axis)
    return lax.ppermute(shard, axis, [(i, i ^ bit) for i in range(devices)])


def step_bits(devices):
    bits = []
    bit = devices // 2
    while bit:
        bits.append(bit)
        bit //= 2
    return bits


def slot_offsets(devices):
    offsets = [0]
    for bit in step_bits(devices):
        offsets = offsets + [item ^ bit for item in offsets]
    return offsets


def gather_slots(shard, axis):
    gathered = shard[None]
    for bit in step_bits(lax.axis_size(axis)):
        gathered = jnp.concatenate([gathered, swapped(gathered, axis, bit)], axis=0)
    return gathered


def scatter_slots(slots, axis):
    current = slots
    for bit in reversed(step_bits(lax.axis_size(axis))):
        half = current.shape[0] // 2
        arrived = swapped(current[half:], axis, bit)
        summed = current[:half].astype(jnp.float32) + arrived.astype(jnp.float32)
        current = summed.astype(jnp.bfloat16) if bit * 2 < lax.axis_size(axis) else summed
    return current[0]


def tp_sum(part):
    if lax.axis_size("tp") == 2:
        return part.astype(jnp.float32) + swapped(part, "tp", 1).astype(jnp.float32)
    return lax.psum(part, "tp").astype(jnp.float32)


def product(left, right):
    return jnp.dot(left, right, preferred_element_type=jnp.float32)


def norm_rows(values):
    factor = lax.rsqrt(jnp.mean(values * values, axis=-1, keepdims=True) + EPS)
    return (values * factor, factor)


def norm_back(gradient, normed, factor, gain):
    scaled = gradient * gain
    return factor * (scaled - normed * jnp.mean(scaled * normed, axis=-1, keepdims=True))


def rotate(values, cosine, sine_part):
    half_dim = values.shape[-1] // 2
    first_half = values[..., :half_dim]
    second_half = values[..., half_dim:]
    return jnp.concatenate(
        [
            first_half * cosine - second_half * sine_part,
            second_half * cosine + first_half * sine_part,
        ],
        axis=-1,
    )


def to_heads(flattened, sequences, key_heads, group_size):
    row_count = flattened.size // (sequences * key_heads * group_size * DH)
    arranged = flattened.reshape(sequences, row_count, key_heads, group_size, DH)
    return arranged.transpose(0, 2, 3, 1, 4).reshape(
        sequences, key_heads, group_size * row_count, DH
    )


def from_heads(stacked, group_size):
    sequences = stacked.shape[0]
    key_heads = stacked.shape[1]
    row_count = stacked.shape[2] // group_size
    arranged = stacked.reshape(sequences, key_heads, group_size, row_count, DH).transpose(
        0, 3, 1, 2, 4
    )
    return arranged.reshape(sequences * row_count, key_heads * group_size * DH)


def softmax_block(query_ref, pair_ref, query_place_ref, key_place_ref):
    pair = pair_ref[...]
    pair = pair.reshape(pair.shape[0] * pair.shape[3], pair.shape[4])
    key_rows = pair[:, :DH]
    value_rows = pair[:, DH:]
    query_rows = query_ref[0, 0] * SCALE
    scores = lax.dot_general(
        query_rows, key_rows, (((1,), (1,)), ((), ())), preferred_element_type=jnp.float32
    )
    scores = jnp.where(key_place_ref[0] <= query_place_ref[0], scores, -1e30)
    weights = jnp.exp(scores - jnp.max(scores, axis=-1, keepdims=True))
    weights = weights * (1.0 / jnp.sum(weights, axis=-1, keepdims=True))
    return query_rows, key_rows, value_rows, weights


def attend_kernel(query_ref, pair_ref, query_place_ref, key_place_ref, out_ref):
    unused_query, unused_key, value_rows, weights = softmax_block(
        query_ref, pair_ref, query_place_ref, key_place_ref
    )
    out_ref[0, 0] = product(weights.astype(jnp.bfloat16), value_rows).astype(out_ref.dtype)


def attend_back_kernel(
    query_ref, pair_ref, query_place_ref, key_place_ref, grad_ref, query_grad_ref, pair_grad_ref
):
    query_rows, key_rows, value_rows, weights = softmax_block(
        query_ref, pair_ref, query_place_ref, key_place_ref
    )
    grad_rows = grad_ref[0, 0]
    weight_grad = lax.dot_general(
        grad_rows, value_rows, (((1,), (1,)), ((), ())), preferred_element_type=jnp.float32
    )
    delta = jnp.sum(weights * weight_grad, axis=-1, keepdims=True)
    score_grad = (weights * (weight_grad - delta)).astype(jnp.bfloat16)
    query_grad_ref[0, 0] = product(score_grad, key_rows) * SCALE
    across = (((0,), (0,)), ((), ()))
    key_grad = lax.dot_general(
        score_grad, query_rows, across, preferred_element_type=jnp.float32
    )
    value_grad = lax.dot_general(
        weights.astype(jnp.bfloat16), grad_rows, across, preferred_element_type=jnp.float32
    )
    pair_grad = jnp.concatenate([key_grad, value_grad], axis=-1).astype(pair_grad_ref.dtype)
    pair_grad_ref[...] = pair_grad.reshape(pair_grad_ref.shape)


def attend_call(kernel, arrays, out_shapes, transcendentals):
    queries, pairs = arrays[0], arrays[1]
    sequences, key_heads, query_rows, unused = queries.shape
    slots, seq_rows = pairs.shape[0], pairs.shape[3]
    key_rows = slots * seq_rows

    def spec_of(array):
        if len(array.shape) == 5:
            return pl.BlockSpec((slots, 1, 1, seq_rows, 2 * DH), lambda s, h: (0, s, h, 0, 0))
        return pl.BlockSpec((1, 1, query_rows, DH), lambda s, h: (s, h, 0, 0))

    place_specs = [
        pl.BlockSpec((1, query_rows, 1), lambda s, h: (s, 0, 0)),
        pl.BlockSpec((1, 1, key_rows), lambda s, h: (s, 0, 0)),
    ]
    work = sequences * key_heads * query_rows * key_rows
    return pl.pallas_call(
        kernel,
        grid=(sequences, key_heads),
        in_specs=[spec_of(queries), spec_of(pairs)]
        + place_specs
        + [spec_of(array) for array in arrays[4:]],
        out_specs=[spec_of(shape) for shape in out_shapes],
        out_shape=out_shapes,
        compiler_params=pltpu.CompilerParams(vmem_limit_bytes=VMEM_LIMIT),
        cost_estimate=pl.CostEstimate(
            flops=4 * DH * work * transcendentals,
            bytes_accessed=4 * pairs.size,
            transcendentals=work,
        ),
    )(*arrays)


def shards(
    states,
    span_order,
    attn_gain,
    w_query,
    w_key,
    w_value,
    query_gain,
    key_gain,
    w_out,
    ffn_gain,
    w_gate,
    w_up,
    w_down,
    grad_out,
):
    ctx_count = lax.axis_size("ctx")
    own_index = lax.axis_index("ctx")
    token_rows, width = states.shape
    sequences = span_order.shape[1] // 2
    seq_rows = token_rows // sequences
    span_len = seq_rows // 2
    shard_rows = w_query.shape[0]
    query_cols = w_query.shape[1]
    key_cols = w_key.shape[1]
    query_heads = query_cols // DH
    key_heads = key_cols // DH
    group_size = query_heads // key_heads
    gain_part = query_gain.shape[0]
    attn_cols = query_cols + 2 * key_cols

    owners = own_index ^ jnp.array(slot_offsets(ctx_count), jnp.int32)
    source_column = (owners[:, None] * shard_rows + jnp.arange(shard_rows)[None, :]).reshape(width)
    to_slots = (jnp.arange(width)[:, None] == source_column[None, :]).astype(jnp.bfloat16)
    states_slots = product(states, to_slots).astype(jnp.bfloat16)
    grad_out_slots = product(grad_out, to_slots).astype(jnp.bfloat16)

    packed_cols = attn_cols + query_cols
    small = jnp.concatenate(
        [attn_gain, ffn_gain, query_gain, key_gain, span_order[0].astype(jnp.bfloat16)]
    )
    small_rows = jnp.pad(small[None, :], ((0, EXTRA_ROWS - 1), (0, packed_cols - small.shape[0])))
    packed = jnp.concatenate(
        [jnp.concatenate([w_query, w_key, w_value, w_out.T], axis=1), small_rows], axis=0
    )
    gathered = gather_slots(packed, "ctx")
    qkv_full = gathered[:, :shard_rows, :attn_cols].reshape(width, attn_cols)
    out_full = gathered[:, :shard_rows, attn_cols:].reshape(width, query_cols)
    small_full = gathered[:, shard_rows, : small.shape[0]]
    ends = [shard_rows, 2 * shard_rows, 2 * shard_rows + gain_part, 2 * shard_rows + 2 * gain_part]
    gain_attn = small_full[:, : ends[0]].reshape(width).astype(jnp.float32)
    gain_ffn = small_full[:, ends[0] : ends[1]].reshape(width).astype(jnp.float32)
    by_owner = (jnp.arange(ctx_count)[:, None] == owners[None, :]).astype(jnp.float32)
    gain_query = jnp.sum(
        by_owner[:, :, None] * small_full[None, :, ends[1] : ends[2]].astype(jnp.float32), axis=1
    ).reshape(DH)
    gain_key = jnp.sum(
        by_owner[:, :, None] * small_full[None, :, ends[2] : ends[3]].astype(jnp.float32), axis=1
    ).reshape(DH)
    order_slots = small_full[:, ends[3] :].astype(jnp.int32)
    offsets = jnp.arange(span_len, dtype=jnp.int32)
    every_place = (order_slots.reshape(ctx_count, sequences, 2, 1) * span_len + offsets).reshape(
        ctx_count, sequences, seq_rows
    )
    own_place = every_place[0]
    key_place = jnp.transpose(every_place, (1, 0, 2)).reshape(sequences, 1, ctx_count * seq_rows)
    query_place = jnp.tile(own_place, (1, group_size))[:, :, None]

    w_gate, w_up, w_down, qkv_full = lax.optimization_barrier((w_gate, w_up, w_down, qkv_full))
    gate_full = gather_slots(w_gate, "ctx").reshape(width, -1)
    up_full = gather_slots(w_up, "ctx").reshape(width, -1)
    down_full = gather_slots(w_down.T, "ctx").reshape(width, -1)

    inputs = states_slots.astype(jnp.float32)
    normed_one, factor_one = norm_rows(inputs)
    hidden_one = (normed_one * gain_attn).astype(jnp.bfloat16)
    qkv = product(hidden_one, qkv_full)
    query_pre = qkv[:, :query_cols].reshape(token_rows, query_heads, DH)
    key_pre = qkv[:, query_cols : query_cols + key_cols].reshape(token_rows, key_heads, DH)
    value_low = qkv[:, query_cols + key_cols :].astype(jnp.bfloat16)
    half_dim = DH // 2
    inverse_freq = jnp.exp(-math.log(THETA) * jnp.arange(half_dim, dtype=jnp.float32) / half_dim)
    angles = own_place.reshape(token_rows).astype(jnp.float32)[:, None] * inverse_freq[None, :]
    cosine = jnp.cos(angles)[:, None, :]
    sine_part = jnp.sin(angles)[:, None, :]
    query_normed, query_factor = norm_rows(query_pre)
    key_normed, key_factor = norm_rows(key_pre)
    query_rot = rotate(query_normed * gain_query, cosine, sine_part).astype(jnp.bfloat16)
    key_rot = rotate(key_normed * gain_key, cosine, sine_part).astype(jnp.bfloat16)
    queries = to_heads(query_rot, sequences, key_heads, group_size)
    keys = to_heads(key_rot, sequences, key_heads, 1)
    values = to_heads(value_low, sequences, key_heads, 1)
    pairs = gather_slots(jnp.concatenate([keys, values], axis=-1), "ctx")
    attend_inputs = (queries, pairs, query_place, key_place)
    (attended,) = attend_call(
        attend_kernel, attend_inputs, [jax.ShapeDtypeStruct(queries.shape, jnp.bfloat16)], 1
    )
    mixed_low = from_heads(attended, group_size)
    attn_terms = jnp.einsum("ta,da->td", mixed_low, out_full, preferred_element_type=jnp.float32)
    middle = inputs + tp_sum(attn_terms.astype(jnp.bfloat16))
    normed_two, factor_two = norm_rows(middle)
    hidden_two = (normed_two * gain_ffn).astype(jnp.bfloat16)
    gate_proj = product(hidden_two, gate_full)
    up_proj = product(hidden_two, up_full)
    sigmoid_gate = 1.0 / (1.0 + jnp.exp(-gate_proj))
    activated = gate_proj * sigmoid_gate
    inner = (activated * up_proj).astype(jnp.bfloat16)
    slotted = lambda grad: grad.astype(jnp.bfloat16).reshape(ctx_count, shard_rows, -1)
    down_grad = jnp.einsum("td,tf->df", grad_out_slots, inner, preferred_element_type=jnp.float32)
    down_share = scatter_slots(slotted(down_grad), "ctx")
    inner_grad = product(grad_out_slots, down_full)
    gate_grad = (
        inner_grad * up_proj * sigmoid_gate * (1.0 + gate_proj * (1.0 - sigmoid_gate))
    ).astype(jnp.bfloat16)
    up_grad = (inner_grad * activated).astype(jnp.bfloat16)
    hidden_two_part = jnp.einsum(
        "tf,cf->tc", gate_grad, gate_full, preferred_element_type=jnp.float32
    ) + jnp.einsum("tf,cf->tc", up_grad, up_full, preferred_element_type=jnp.float32)
    hidden_two_grad = tp_sum(hidden_two_part.astype(jnp.bfloat16))
    gate_wgrad = jnp.einsum("tc,tf->cf", hidden_two, gate_grad, preferred_element_type=jnp.float32)
    gate_share = scatter_slots(slotted(gate_wgrad), "ctx")
    up_wgrad = jnp.einsum("tc,tf->cf", hidden_two, up_grad, preferred_element_type=jnp.float32)
    up_share = scatter_slots(slotted(up_wgrad), "ctx")
    ffn_terms = jnp.einsum("tf,df->td", inner, down_full, preferred_element_type=jnp.float32)
    output_slots = (middle + tp_sum(ffn_terms.astype(jnp.bfloat16))).astype(jnp.bfloat16)
    output_low = jnp.einsum(
        "td,ed->te", output_slots, to_slots, preferred_element_type=jnp.float32
    ).astype(jnp.bfloat16)
    ffn_gain_grad = jnp.sum(hidden_two_grad * normed_two, axis=0)
    middle_grad = grad_out_slots.astype(jnp.float32) + norm_back(
        hidden_two_grad, normed_two, factor_two, gain_ffn
    )
    branch_low = middle_grad.astype(jnp.bfloat16)
    out_wgrad = jnp.einsum("td,ta->da", branch_low, mixed_low, preferred_element_type=jnp.float32)
    mixed_grad = product(branch_low, out_full).astype(jnp.bfloat16)
    attended_grad = to_heads(mixed_grad, sequences, key_heads, group_size)
    query_grad, pair_grad = attend_call(
        attend_back_kernel,
        attend_inputs + (attended_grad,),
        [
            jax.ShapeDtypeStruct(queries.shape, jnp.float32),
            jax.ShapeDtypeStruct(pairs.shape, jnp.bfloat16),
        ],
        3,
    )
    pair_share = scatter_slots(pair_grad, "ctx")
    query_rot_grad = from_heads(query_grad, group_size).reshape(token_rows, query_heads, DH)
    key_rot_grad = from_heads(pair_share[..., :DH], 1).reshape(token_rows, key_heads, DH)
    value_grad_low = from_heads(pair_share[..., DH:], 1).astype(jnp.bfloat16)
    query_out_grad = rotate(query_rot_grad, cosine, -sine_part)
    key_out_grad = rotate(key_rot_grad, cosine, -sine_part)
    query_gain_grad = jnp.sum(query_out_grad * query_normed, axis=(0, 1))
    key_gain_grad = jnp.sum(key_out_grad * key_normed, axis=(0, 1))
    query_pre_grad = norm_back(query_out_grad, query_normed, query_factor, gain_query)
    key_pre_grad = norm_back(key_out_grad, key_normed, key_factor, gain_key)
    qkv_grad = jnp.concatenate(
        [
            query_pre_grad.reshape(token_rows, query_cols).astype(jnp.bfloat16),
            key_pre_grad.reshape(token_rows, key_cols).astype(jnp.bfloat16),
            value_grad_low,
        ],
        axis=1,
    )
    hidden_one_part = jnp.einsum(
        "ta,ca->tc", qkv_grad, qkv_full, preferred_element_type=jnp.float32
    )
    gain_terms = jnp.concatenate([query_gain_grad, key_gain_grad])[None, :]
    gain_rows = jnp.pad(gain_terms, ((0, EXTRA_ROWS - 1), (0, width - gain_terms.shape[1])))
    summed = tp_sum(jnp.concatenate([hidden_one_part, gain_rows], axis=0).astype(jnp.bfloat16))
    qkv_wgrad = jnp.einsum("tc,ta->ca", hidden_one, qkv_grad, preferred_element_type=jnp.float32)
    hidden_one_grad = summed[:token_rows]
    attn_gain_grad = jnp.sum(hidden_one_grad * normed_one, axis=0)
    states_slots_grad = middle_grad + norm_back(
        hidden_one_grad, normed_one, factor_one, gain_attn
    )
    states_grad = jnp.einsum(
        "td,ed->te",
        states_slots_grad,
        to_slots.astype(jnp.float32),
        precision=lax.Precision.HIGHEST,
        preferred_element_type=jnp.float32,
    )
    gain_sums = summed[token_rows, : 2 * DH].reshape(2, ctx_count, gain_part)
    gain_slots = jnp.sum(by_owner[None, :, :, None] * gain_sums[:, :, None, :], axis=1)
    small_grads = jnp.concatenate(
        [
            attn_gain_grad.reshape(ctx_count, shard_rows),
            ffn_gain_grad.reshape(ctx_count, shard_rows),
            gain_slots[0],
            gain_slots[1],
        ],
        axis=1,
    ).astype(jnp.bfloat16)
    small_share = scatter_slots(small_grads[:, None, :], "ctx")[0]
    attn_share = scatter_slots(
        slotted(jnp.concatenate([qkv_wgrad, out_wgrad], axis=1)), "ctx"
    )
    return (
        output_low,
        states_grad,
        small_share[: ends[0]],
        attn_share[:, :query_cols],
        attn_share[:, query_cols : query_cols + key_cols],
        attn_share[:, query_cols + key_cols : attn_cols],
        small_share[ends[1] : ends[2]],
        small_share[ends[2] : ends[3]],
        attn_share[:, attn_cols:].T,
        small_share[ends[0] : ends[1]],
        gate_share,
        up_share,
        down_share.T,
    )


def solution(mesh):
    in_specs = (
        P("ctx", None),
        P("ctx", None),
        P("ctx"),
        P("ctx", "tp"),
        P("ctx", "tp"),
        P("ctx", "tp"),
        P("ctx"),
        P("ctx"),
        P("tp", "ctx"),
        P("ctx"),
        P("ctx", "tp"),
        P("ctx", "tp"),
        P("tp", "ctx"),
        P("ctx", None),
    )
    out_specs = (
        P("ctx", None),
        P("ctx", None),
        P("ctx"),
        P("ctx", "tp"),
        P("ctx", "tp"),
        P("ctx", "tp"),
        P("ctx"),
        P("ctx"),
        P("tp", "ctx"),
        P("ctx"),
        P("ctx", "tp"),
        P("ctx", "tp"),
        P("tp", "ctx"),
    )
    return jax.shard_map(shards, mesh=mesh, in_specs=in_specs, out_specs=out_specs, check_vma=False)
```

```python
import math

import jax
import jax.numpy as jnp
from jax import lax
from jax.experimental import pallas as pl
from jax.experimental.pallas import tpu as pltpu
from jax.sharding import PartitionSpec as P

DH = 64


EPS = 1e-05
THETA = 1000000.0
SCALE = 0.125


VMEM_LIMIT = 48 * 1024 * 1024
EXTRA_ROWS = 16


def swapped(shard, axis, bit):
    devices = lax.axis_size(axis)
    return lax.ppermute(shard, axis, [(i, i ^ bit) for i in range(devices)])


def step_bits(devices):
    bits = []
    bit = devices // 2
    while bit:
        bits.append(bit)
        bit //= 2
    return bits


def slot_offsets(devices):
    offsets = [0]
    for bit in step_bits(devices):
        offsets = offsets + [item ^ bit for item in offsets]
    return offsets


def after(value, *earlier):
    return lax.optimization_barrier((value,) + earlier)[0]


def gather_step(gathered, axis, bit):
    return jnp.concatenate([gathered, swapped(gathered, axis, bit)], axis=0)


def gather_outer(shard, axis):
    gathered = shard[None]
    for bit in step_bits(lax.axis_size(axis))[:-2]:
        gathered = gather_step(gathered, axis, bit)
    return gathered


def halves_of(slots):
    half = slots.shape[0] // 2
    return slots[:half], slots[half:]


def added(kept, arrived):
    return (kept.astype(jnp.float32) + arrived.astype(jnp.float32)).astype(jnp.bfloat16)


def scatter_core(slots, axis):
    kept, sent = halves_of(slots)
    return added(kept, swapped(sent, axis, 1))


def scatter_outer(slots, axis):
    current = slots
    for bit in reversed(step_bits(lax.axis_size(axis))[:-2]):
        kept, sent = halves_of(current)
        arrived = swapped(sent, axis, bit)
        current = added(kept, arrived)
    return kept[0].astype(jnp.float32) + arrived[0].astype(jnp.float32)


def tp_sum(part):
    if lax.axis_size("tp") == 2:
        return part.astype(jnp.float32) + swapped(part, "tp", 1).astype(jnp.float32)
    return lax.psum(part, "tp").astype(jnp.float32)


def product(left, right):
    return jnp.dot(left, right, preferred_element_type=jnp.float32)


def norm_rows(values):
    factor = lax.rsqrt(jnp.mean(values * values, axis=-1, keepdims=True) + EPS)
    return (values * factor, factor)


def norm_back(gradient, normed, factor, gain):
    scaled = gradient * gain
    return factor * (scaled - normed * jnp.mean(scaled * normed, axis=-1, keepdims=True))


def rotate(values, cosine, sine_part):
    half_dim = values.shape[-1] // 2
    first_half = values[..., :half_dim]
    second_half = values[..., half_dim:]
    return jnp.concatenate(
        [
            first_half * cosine - second_half * sine_part,
            second_half * cosine + first_half * sine_part,
        ],
        axis=-1,
    )


def to_heads(flattened, sequences, key_heads, group_size):
    row_count = flattened.size // (sequences * key_heads * group_size * DH)
    arranged = flattened.reshape(sequences, row_count, key_heads, group_size, DH)
    return arranged.transpose(0, 2, 3, 1, 4).reshape(
        sequences, key_heads, group_size * row_count, DH
    )


def from_heads(stacked, group_size):
    sequences = stacked.shape[0]
    key_heads = stacked.shape[1]
    row_count = stacked.shape[2] // group_size
    arranged = stacked.reshape(sequences, key_heads, group_size, row_count, DH).transpose(
        0, 3, 1, 2, 4
    )
    return arranged.reshape(sequences * row_count, key_heads * group_size * DH)


def softmax_block(query_ref, pair_ref, query_place_ref, key_place_ref):
    pair = pair_ref[...]
    pair = pair.reshape(pair.shape[0] * pair.shape[3], pair.shape[4])
    key_rows = pair[:, :DH]
    value_rows = pair[:, DH:]
    query_rows = query_ref[0, 0] * SCALE
    scores = lax.dot_general(
        query_rows, key_rows, (((1,), (1,)), ((), ())), preferred_element_type=jnp.float32
    )
    scores = jnp.where(key_place_ref[0] <= query_place_ref[0], scores, -1e30)
    weights = jnp.exp(scores - jnp.max(scores, axis=-1, keepdims=True))
    weights = weights * (1.0 / jnp.sum(weights, axis=-1, keepdims=True))
    return query_rows, key_rows, value_rows, weights


def attend_kernel(query_ref, pair_ref, query_place_ref, key_place_ref, out_ref):
    unused_query, unused_key, value_rows, weights = softmax_block(
        query_ref, pair_ref, query_place_ref, key_place_ref
    )
    out_ref[0, 0] = product(weights.astype(jnp.bfloat16), value_rows).astype(out_ref.dtype)


def attend_back_kernel(
    query_ref, pair_ref, query_place_ref, key_place_ref, grad_ref, query_grad_ref, pair_grad_ref
):
    query_rows, key_rows, value_rows, weights = softmax_block(
        query_ref, pair_ref, query_place_ref, key_place_ref
    )
    grad_rows = grad_ref[0, 0]
    weight_grad = lax.dot_general(
        grad_rows, value_rows, (((1,), (1,)), ((), ())), preferred_element_type=jnp.float32
    )
    delta = jnp.sum(weights * weight_grad, axis=-1, keepdims=True)
    score_grad = (weights * (weight_grad - delta)).astype(jnp.bfloat16)
    query_grad_ref[0, 0] = product(score_grad, key_rows) * SCALE
    across = (((0,), (0,)), ((), ()))
    key_grad = lax.dot_general(
        score_grad, query_rows, across, preferred_element_type=jnp.float32
    )
    value_grad = lax.dot_general(
        weights.astype(jnp.bfloat16), grad_rows, across, preferred_element_type=jnp.float32
    )
    pair_grad = jnp.concatenate([key_grad, value_grad], axis=-1).astype(pair_grad_ref.dtype)
    pair_grad_ref[...] = pair_grad.reshape(pair_grad_ref.shape)


def attend_call(kernel, arrays, out_shapes, transcendentals):
    queries, pairs = arrays[0], arrays[1]
    sequences, key_heads, query_rows, unused = queries.shape
    slots, seq_rows = pairs.shape[0], pairs.shape[3]
    key_rows = slots * seq_rows

    def spec_of(array):
        if len(array.shape) == 5:
            return pl.BlockSpec((slots, 1, 1, seq_rows, 2 * DH), lambda s, h: (0, s, h, 0, 0))
        return pl.BlockSpec((1, 1, query_rows, DH), lambda s, h: (s, h, 0, 0))

    place_specs = [
        pl.BlockSpec((1, query_rows, 1), lambda s, h: (s, 0, 0)),
        pl.BlockSpec((1, 1, key_rows), lambda s, h: (s, 0, 0)),
    ]
    work = sequences * key_heads * query_rows * key_rows
    return pl.pallas_call(
        kernel,
        grid=(sequences, key_heads),
        in_specs=[spec_of(queries), spec_of(pairs)]
        + place_specs
        + [spec_of(array) for array in arrays[4:]],
        out_specs=[spec_of(shape) for shape in out_shapes],
        out_shape=out_shapes,
        compiler_params=pltpu.CompilerParams(vmem_limit_bytes=VMEM_LIMIT),
        cost_estimate=pl.CostEstimate(
            flops=4 * DH * work * transcendentals,
            bytes_accessed=4 * pairs.size,
            transcendentals=work,
        ),
    )(*arrays)


def shards(
    states,
    span_order,
    attn_gain,
    w_query,
    w_key,
    w_value,
    query_gain,
    key_gain,
    w_out,
    ffn_gain,
    w_gate,
    w_up,
    w_down,
    grad_out,
):
    ctx_count = lax.axis_size("ctx")
    own_index = lax.axis_index("ctx")
    token_rows, width = states.shape
    sequences = span_order.shape[1] // 2
    seq_rows = token_rows // sequences
    span_len = seq_rows // 2
    shard_rows = w_query.shape[0]
    query_cols = w_query.shape[1]
    key_cols = w_key.shape[1]
    query_heads = query_cols // DH
    key_heads = key_cols // DH
    group_size = query_heads // key_heads
    gain_part = query_gain.shape[0]
    attn_cols = query_cols + 2 * key_cols

    owners = own_index ^ jnp.array(slot_offsets(ctx_count), jnp.int32)
    source_column = (owners[:, None] * shard_rows + jnp.arange(shard_rows)[None, :]).reshape(width)
    to_slots = (jnp.arange(width)[:, None] == source_column[None, :]).astype(jnp.bfloat16)
    states_slots = product(states, to_slots).astype(jnp.bfloat16)
    grad_out_slots = product(grad_out, to_slots).astype(jnp.bfloat16)

    packed_cols = attn_cols + query_cols
    small = jnp.concatenate(
        [attn_gain, ffn_gain, query_gain, key_gain, span_order[0].astype(jnp.bfloat16)]
    )
    small_rows = jnp.pad(small[None, :], ((0, EXTRA_ROWS - 1), (0, packed_cols - small.shape[0])))
    packed = jnp.concatenate(
        [jnp.concatenate([w_query, w_key, w_value, w_out.T], axis=1), small_rows], axis=0
    )
    packed_outer = gather_outer(packed, "ctx")
    gate_outer = gather_outer(after(w_gate, packed_outer), "ctx")
    up_outer = gather_outer(after(w_up, gate_outer), "ctx")
    packed_inner = gather_step(packed_outer, "ctx", 2)
    gathered = gather_step(packed_inner, "ctx", 1)
    gate_inner = gather_step(after(gate_outer, packed_inner), "ctx", 2)
    qkv_full = gathered[:, :shard_rows, :attn_cols].reshape(width, attn_cols)
    out_full = gathered[:, :shard_rows, attn_cols:].reshape(width, query_cols)
    small_full = gathered[:, shard_rows, : small.shape[0]]
    ends = [shard_rows, 2 * shard_rows, 2 * shard_rows + gain_part, 2 * shard_rows + 2 * gain_part]
    gain_attn = small_full[:, : ends[0]].reshape(width).astype(jnp.float32)
    gain_ffn = small_full[:, ends[0] : ends[1]].reshape(width).astype(jnp.float32)
    by_owner = (jnp.arange(ctx_count)[:, None] == owners[None, :]).astype(jnp.float32)
    gain_query = jnp.sum(
        by_owner[:, :, None] * small_full[None, :, ends[1] : ends[2]].astype(jnp.float32), axis=1
    ).reshape(DH)
    gain_key = jnp.sum(
        by_owner[:, :, None] * small_full[None, :, ends[2] : ends[3]].astype(jnp.float32), axis=1
    ).reshape(DH)
    order_slots = small_full[:, ends[3] :].astype(jnp.int32)
    offsets = jnp.arange(span_len, dtype=jnp.int32)
    every_place = (order_slots.reshape(ctx_count, sequences, 2, 1) * span_len + offsets).reshape(
        ctx_count, sequences, seq_rows
    )
    own_place = every_place[0]
    key_place = jnp.transpose(every_place, (1, 0, 2)).reshape(sequences, 1, ctx_count * seq_rows)
    query_place = jnp.tile(own_place, (1, group_size))[:, :, None]

    inputs = states_slots.astype(jnp.float32)
    normed_one, factor_one = norm_rows(inputs)
    hidden_one = (normed_one * gain_attn).astype(jnp.bfloat16)
    qkv = product(hidden_one, qkv_full)
    query_pre = qkv[:, :query_cols].reshape(token_rows, query_heads, DH)
    key_pre = qkv[:, query_cols : query_cols + key_cols].reshape(token_rows, key_heads, DH)
    value_low = qkv[:, query_cols + key_cols :].astype(jnp.bfloat16)
    half_dim = DH // 2
    inverse_freq = jnp.exp(-math.log(THETA) * jnp.arange(half_dim, dtype=jnp.float32) / half_dim)
    angles = own_place.reshape(token_rows).astype(jnp.float32)[:, None] * inverse_freq[None, :]
    cosine = jnp.cos(angles)[:, None, :]
    sine_part = jnp.sin(angles)[:, None, :]
    query_normed, query_factor = norm_rows(query_pre)
    key_normed, key_factor = norm_rows(key_pre)
    query_rot = rotate(query_normed * gain_query, cosine, sine_part).astype(jnp.bfloat16)
    key_rot = rotate(key_normed * gain_key, cosine, sine_part).astype(jnp.bfloat16)
    queries = to_heads(query_rot, sequences, key_heads, group_size)
    keys = to_heads(key_rot, sequences, key_heads, 1)
    values = to_heads(value_low, sequences, key_heads, 1)
    pairs_outer = gather_outer(jnp.concatenate([keys, values], axis=-1), "ctx")
    pairs_inner = gather_step(after(pairs_outer, gate_inner), "ctx", 2)
    pairs = gather_step(pairs_inner, "ctx", 1)
    up_sent = after(up_outer, pairs_inner)
    up_arrived = swapped(up_sent, "ctx", 2)
    down_outer = gather_outer(after(w_down.T, pairs_outer), "ctx")
    down_sent = after(down_outer, up_arrived)
    down_arrived = swapped(down_sent, "ctx", 2)
    attend_inputs = (queries, pairs, query_place, key_place)
    (attended,) = attend_call(
        attend_kernel, attend_inputs, [jax.ShapeDtypeStruct(queries.shape, jnp.bfloat16)], 1
    )
    gate_full = gather_step(after(gate_inner, attended), "ctx", 1).reshape(width, -1)
    up_inner = jnp.concatenate([up_sent, after(up_arrived, attended)], axis=0)
    up_full = gather_step(up_inner, "ctx", 1).reshape(width, -1)
    mixed_low = from_heads(attended, group_size)
    attn_terms = jnp.einsum("ta,da->td", mixed_low, out_full, preferred_element_type=jnp.float32)
    middle = inputs + tp_sum(attn_terms.astype(jnp.bfloat16))
    normed_two, factor_two = norm_rows(middle)
    down_inner = jnp.concatenate([down_sent, after(down_arrived, normed_two)], axis=0)
    down_full = gather_step(down_inner, "ctx", 1).reshape(width, -1)
    hidden_two = (normed_two * gain_ffn).astype(jnp.bfloat16)
    gate_proj = product(hidden_two, gate_full)
    up_proj = product(hidden_two, up_full)
    sigmoid_gate = 1.0 / (1.0 + jnp.exp(-gate_proj))
    activated = gate_proj * sigmoid_gate
    inner = (activated * up_proj).astype(jnp.bfloat16)
    slotted = lambda grad: grad.astype(jnp.bfloat16).reshape(ctx_count, shard_rows, -1)
    down_grad = jnp.einsum("td,tf->df", grad_out_slots, inner, preferred_element_type=jnp.float32)
    down_kept, down_sent = halves_of(scatter_core(slotted(down_grad), "ctx"))
    down_arrived = swapped(down_sent, "ctx", 2)
    inner_grad = product(grad_out_slots, down_full)
    gate_grad = (
        inner_grad * up_proj * sigmoid_gate * (1.0 + gate_proj * (1.0 - sigmoid_gate))
    ).astype(jnp.bfloat16)
    up_grad = (inner_grad * activated).astype(jnp.bfloat16)
    hidden_two_part = jnp.einsum(
        "tf,cf->tc", after(gate_grad, down_sent), gate_full, preferred_element_type=jnp.float32
    ) + jnp.einsum("tf,cf->tc", up_grad, up_full, preferred_element_type=jnp.float32)
    hidden_two_grad = tp_sum(hidden_two_part.astype(jnp.bfloat16))
    gate_wgrad = jnp.einsum("tc,tf->cf", hidden_two, gate_grad, preferred_element_type=jnp.float32)
    gate_kept, gate_sent = halves_of(scatter_core(slotted(gate_wgrad), "ctx"))
    gate_arrived = swapped(after(gate_sent, down_arrived), "ctx", 2)
    up_wgrad = jnp.einsum("tc,tf->cf", hidden_two, up_grad, preferred_element_type=jnp.float32)
    up_kept, up_sent = halves_of(scatter_core(slotted(up_wgrad), "ctx"))
    ffn_terms = jnp.einsum("tf,df->td", inner, down_full, preferred_element_type=jnp.float32)
    output_slots = (middle + tp_sum(ffn_terms.astype(jnp.bfloat16))).astype(jnp.bfloat16)
    output_low = jnp.einsum(
        "td,ed->te", output_slots, to_slots, preferred_element_type=jnp.float32
    ).astype(jnp.bfloat16)
    ffn_gain_grad = jnp.sum(hidden_two_grad * normed_two, axis=0)
    middle_grad = grad_out_slots.astype(jnp.float32) + norm_back(
        hidden_two_grad, normed_two, factor_two, gain_ffn
    )
    branch_low = middle_grad.astype(jnp.bfloat16)
    out_wgrad = jnp.einsum("td,ta->da", branch_low, mixed_low, preferred_element_type=jnp.float32)
    mixed_grad = product(branch_low, out_full).astype(jnp.bfloat16)
    down_share = scatter_outer(added(down_kept, after(down_arrived, middle_grad)), "ctx")
    attended_grad = to_heads(after(mixed_grad, gate_sent, down_arrived), sequences, key_heads, group_size)
    query_grad, pair_grad = attend_call(
        attend_back_kernel,
        attend_inputs + (attended_grad,),
        [
            jax.ShapeDtypeStruct(queries.shape, jnp.float32),
            jax.ShapeDtypeStruct(pairs.shape, jnp.bfloat16),
        ],
        3,
    )
    gate_share = scatter_outer(added(gate_kept, after(gate_arrived, pair_grad)), "ctx")
    pair_kept, pair_sent = halves_of(scatter_core(after(pair_grad, gate_arrived), "ctx"))
    pair_arrived = swapped(pair_sent, "ctx", 2)
    pair_share = scatter_outer(added(pair_kept, pair_arrived), "ctx")
    up_arrived = swapped(after(up_sent, gate_arrived, pair_arrived), "ctx", 2)
    query_rot_grad = from_heads(query_grad, group_size).reshape(token_rows, query_heads, DH)
    key_rot_grad = from_heads(pair_share[..., :DH], 1).reshape(token_rows, key_heads, DH)
    value_grad_low = from_heads(pair_share[..., DH:], 1).astype(jnp.bfloat16)
    query_out_grad = rotate(query_rot_grad, cosine, -sine_part)
    key_out_grad = rotate(key_rot_grad, cosine, -sine_part)
    query_gain_grad = jnp.sum(query_out_grad * query_normed, axis=(0, 1))
    key_gain_grad = jnp.sum(key_out_grad * key_normed, axis=(0, 1))
    query_pre_grad = norm_back(query_out_grad, query_normed, query_factor, gain_query)
    key_pre_grad = norm_back(key_out_grad, key_normed, key_factor, gain_key)
    qkv_grad = jnp.concatenate(
        [
            query_pre_grad.reshape(token_rows, query_cols).astype(jnp.bfloat16),
            key_pre_grad.reshape(token_rows, key_cols).astype(jnp.bfloat16),
            value_grad_low,
        ],
        axis=1,
    )
    qkv_grad = after(qkv_grad, up_arrived)
    hidden_one_part = jnp.einsum(
        "ta,ca->tc", qkv_grad, qkv_full, preferred_element_type=jnp.float32
    )
    gain_terms = jnp.concatenate([query_gain_grad, key_gain_grad])[None, :]
    gain_rows = jnp.pad(gain_terms, ((0, EXTRA_ROWS - 1), (0, width - gain_terms.shape[1])))
    summed = tp_sum(jnp.concatenate([hidden_one_part, gain_rows], axis=0).astype(jnp.bfloat16))
    qkv_wgrad = jnp.einsum("tc,ta->ca", hidden_one, qkv_grad, preferred_element_type=jnp.float32)
    hidden_one_grad = summed[:token_rows]
    attn_gain_grad = jnp.sum(hidden_one_grad * normed_one, axis=0)
    states_slots_grad = middle_grad + norm_back(
        hidden_one_grad, normed_one, factor_one, gain_attn
    )
    states_grad = jnp.einsum(
        "td,ed->te",
        states_slots_grad,
        to_slots.astype(jnp.float32),
        precision=lax.Precision.HIGHEST,
        preferred_element_type=jnp.float32,
    )
    gain_sums = summed[token_rows, : 2 * DH].reshape(2, ctx_count, gain_part)
    gain_slots = jnp.sum(by_owner[None, :, :, None] * gain_sums[:, :, None, :], axis=1)
    small_grads = jnp.concatenate(
        [
            attn_gain_grad.reshape(ctx_count, shard_rows),
            ffn_gain_grad.reshape(ctx_count, shard_rows),
            gain_slots[0],
            gain_slots[1],
        ],
        axis=1,
    ).astype(jnp.bfloat16)
    small_rows = jnp.pad(
        small_grads[:, None, :],
        ((0, 0), (0, EXTRA_ROWS - 1), (0, packed_cols - small_grads.shape[1])),
    )
    packed_grad = jnp.concatenate(
        [slotted(jnp.concatenate([qkv_wgrad, out_wgrad], axis=1)), small_rows], axis=1
    )
    packed_kept, packed_sent = halves_of(scatter_core(packed_grad, "ctx"))
    packed_arrived = swapped(after(packed_sent, up_arrived), "ctx", 2)
    up_share = scatter_outer(added(up_kept, after(up_arrived, qkv_grad)), "ctx")
    packed_share = scatter_outer(added(packed_kept, packed_arrived), "ctx")
    attn_share = packed_share[:shard_rows]
    small_share = packed_share[shard_rows]
    return (
        output_low,
        states_grad,
        small_share[: ends[0]],
        attn_share[:, :query_cols],
        attn_share[:, query_cols : query_cols + key_cols],
        attn_share[:, query_cols + key_cols : attn_cols],
        small_share[ends[1] : ends[2]],
        small_share[ends[2] : ends[3]],
        attn_share[:, attn_cols:].T,
        small_share[ends[0] : ends[1]],
        gate_share,
        up_share,
        down_share.T,
    )


def solution(mesh):
    in_specs = (
        P("ctx", None),
        P("ctx", None),
        P("ctx"),
        P("ctx", "tp"),
        P("ctx", "tp"),
        P("ctx", "tp"),
        P("ctx"),
        P("ctx"),
        P("tp", "ctx"),
        P("ctx"),
        P("ctx", "tp"),
        P("ctx", "tp"),
        P("tp", "ctx"),
        P("ctx", None),
    )
    out_specs = (
        P("ctx", None),
        P("ctx", None),
        P("ctx"),
        P("ctx", "tp"),
        P("ctx", "tp"),
        P("ctx", "tp"),
        P("ctx"),
        P("ctx"),
        P("tp", "ctx"),
        P("ctx"),
        P("ctx", "tp"),
        P("ctx", "tp"),
        P("tp", "ctx"),
    )
    return jax.shard_map(shards, mesh=mesh, in_specs=in_specs, out_specs=out_specs, check_vma=False)
```

```python
import math

import jax
import jax.numpy as jnp
from jax import lax
from jax.experimental import pallas as pl
from jax.experimental.pallas import tpu as pltpu
from jax.sharding import PartitionSpec as P

DH = 64


EPS = 1e-05
THETA = 1000000.0
SCALE = 0.125


VMEM_LIMIT = 48 * 1024 * 1024
EXTRA_ROWS = 16


def swapped(shard, axis, bit):
    devices = lax.axis_size(axis)
    return lax.ppermute(shard, axis, [(i, i ^ bit) for i in range(devices)])


def step_bits(devices):
    bits = []
    bit = devices // 2
    while bit:
        bits.append(bit)
        bit //= 2
    return bits


def slot_offsets(devices):
    offsets = [0]
    for bit in step_bits(devices):
        offsets = offsets + [item ^ bit for item in offsets]
    return offsets


def after(value, *earlier):
    return lax.optimization_barrier((value,) + earlier)[0]


def gather_step(gathered, axis, bit):
    return jnp.concatenate([gathered, swapped(gathered, axis, bit)], axis=0)


def gather_rest(sent, arrived, axis):
    gathered = jnp.concatenate([sent, arrived], axis=0)
    for bit in step_bits(lax.axis_size(axis))[1:-2]:
        gathered = gather_step(gathered, axis, bit)
    return gathered


def gather_first(shard, axis):
    return shard[None], swapped(shard[None], axis, lax.axis_size(axis) // 2)


def gather_outer(shard, axis):
    return gather_rest(*gather_first(shard, axis), axis)


def halves_of(slots):
    half = slots.shape[0] // 2
    return slots[:half], slots[half:]


def added(kept, arrived):
    return (kept.astype(jnp.float32) + arrived.astype(jnp.float32)).astype(jnp.bfloat16)


def scatter_step(slots, axis, bit):
    kept, sent = halves_of(slots)
    return kept, swapped(sent, axis, bit)


def scatter_first(slots, axis):
    return scatter_step(slots, axis, 4)


def scatter_last(kept, arrived, axis):
    for bit in reversed(step_bits(lax.axis_size(axis))[:-3]):
        kept, arrived = scatter_step(added(kept, arrived), axis, bit)
    return kept, arrived


def total_of(kept, arrived):
    return kept[0].astype(jnp.float32) + arrived[0].astype(jnp.float32)


def tp_sum(part):
    if lax.axis_size("tp") == 2:
        return part.astype(jnp.float32) + swapped(part, "tp", 1).astype(jnp.float32)
    return lax.psum(part, "tp").astype(jnp.float32)


def product(left, right):
    return jnp.dot(left, right, preferred_element_type=jnp.float32)


def norm_rows(values):
    factor = lax.rsqrt(jnp.mean(values * values, axis=-1, keepdims=True) + EPS)
    return (values * factor, factor)


def norm_back(gradient, normed, factor, gain):
    scaled = gradient * gain
    return factor * (scaled - normed * jnp.mean(scaled * normed, axis=-1, keepdims=True))


def rotate(values, cosine, sine_part):
    half_dim = values.shape[-1] // 2
    first_half = values[..., :half_dim]
    second_half = values[..., half_dim:]
    return jnp.concatenate(
        [
            first_half * cosine - second_half * sine_part,
            second_half * cosine + first_half * sine_part,
        ],
        axis=-1,
    )


def to_heads(flattened, sequences, key_heads, group_size):
    row_count = flattened.size // (sequences * key_heads * group_size * DH)
    arranged = flattened.reshape(sequences, row_count, key_heads, group_size, DH)
    return arranged.transpose(0, 2, 3, 1, 4).reshape(
        sequences, key_heads, group_size * row_count, DH
    )


def from_heads(stacked, group_size):
    sequences = stacked.shape[0]
    key_heads = stacked.shape[1]
    row_count = stacked.shape[2] // group_size
    arranged = stacked.reshape(sequences, key_heads, group_size, row_count, DH).transpose(
        0, 3, 1, 2, 4
    )
    return arranged.reshape(sequences * row_count, key_heads * group_size * DH)


def softmax_block(query_ref, pair_ref, query_place_ref, key_place_ref):
    pair = pair_ref[...]
    pair = pair.reshape(pair.shape[0] * pair.shape[3], pair.shape[4])
    key_rows = pair[:, :DH]
    value_rows = pair[:, DH:]
    query_rows = query_ref[0, 0] * SCALE
    scores = lax.dot_general(
        query_rows, key_rows, (((1,), (1,)), ((), ())), preferred_element_type=jnp.float32
    )
    scores = jnp.where(key_place_ref[0] <= query_place_ref[0], scores, -1e30)
    weights = jnp.exp(scores - jnp.max(scores, axis=-1, keepdims=True))
    weights = weights * (1.0 / jnp.sum(weights, axis=-1, keepdims=True))
    return query_rows, key_rows, value_rows, weights


def attend_kernel(query_ref, pair_ref, query_place_ref, key_place_ref, out_ref):
    unused_query, unused_key, value_rows, weights = softmax_block(
        query_ref, pair_ref, query_place_ref, key_place_ref
    )
    out_ref[0, 0] = product(weights.astype(jnp.bfloat16), value_rows).astype(out_ref.dtype)


def attend_back_kernel(
    query_ref, pair_ref, query_place_ref, key_place_ref, grad_ref, query_grad_ref, pair_grad_ref
):
    query_rows, key_rows, value_rows, weights = softmax_block(
        query_ref, pair_ref, query_place_ref, key_place_ref
    )
    grad_rows = grad_ref[0, 0]
    weight_grad = lax.dot_general(
        grad_rows, value_rows, (((1,), (1,)), ((), ())), preferred_element_type=jnp.float32
    )
    delta = jnp.sum(weights * weight_grad, axis=-1, keepdims=True)
    score_grad = (weights * (weight_grad - delta)).astype(jnp.bfloat16)
    query_grad_ref[0, 0] = product(score_grad, key_rows) * SCALE
    across = (((0,), (0,)), ((), ()))
    key_grad = lax.dot_general(
        score_grad, query_rows, across, preferred_element_type=jnp.float32
    )
    value_grad = lax.dot_general(
        weights.astype(jnp.bfloat16), grad_rows, across, preferred_element_type=jnp.float32
    )
    pair_grad = jnp.concatenate([key_grad, value_grad], axis=-1).astype(pair_grad_ref.dtype)
    pair_grad_ref[...] = pair_grad.reshape(pair_grad_ref.shape)


def attend_call(kernel, arrays, out_shapes, transcendentals):
    queries, pairs = arrays[0], arrays[1]
    sequences, key_heads, query_rows, unused = queries.shape
    slots, seq_rows = pairs.shape[0], pairs.shape[3]
    key_rows = slots * seq_rows

    def spec_of(array):
        if len(array.shape) == 5:
            return pl.BlockSpec((slots, 1, 1, seq_rows, 2 * DH), lambda s, h: (0, s, h, 0, 0))
        return pl.BlockSpec((1, 1, query_rows, DH), lambda s, h: (s, h, 0, 0))

    place_specs = [
        pl.BlockSpec((1, query_rows, 1), lambda s, h: (s, 0, 0)),
        pl.BlockSpec((1, 1, key_rows), lambda s, h: (s, 0, 0)),
    ]
    work = sequences * key_heads * query_rows * key_rows
    return pl.pallas_call(
        kernel,
        grid=(sequences, key_heads),
        in_specs=[spec_of(queries), spec_of(pairs)]
        + place_specs
        + [spec_of(array) for array in arrays[4:]],
        out_specs=[spec_of(shape) for shape in out_shapes],
        out_shape=out_shapes,
        compiler_params=pltpu.CompilerParams(vmem_limit_bytes=VMEM_LIMIT),
        cost_estimate=pl.CostEstimate(
            flops=4 * DH * work * transcendentals,
            bytes_accessed=4 * pairs.size,
            transcendentals=work,
        ),
    )(*arrays)


def shards(
    states,
    span_order,
    attn_gain,
    w_query,
    w_key,
    w_value,
    query_gain,
    key_gain,
    w_out,
    ffn_gain,
    w_gate,
    w_up,
    w_down,
    grad_out,
):
    ctx_count = lax.axis_size("ctx")
    own_index = lax.axis_index("ctx")
    token_rows, width = states.shape
    sequences = span_order.shape[1] // 2
    seq_rows = token_rows // sequences
    span_len = seq_rows // 2
    shard_rows = w_query.shape[0]
    query_cols = w_query.shape[1]
    key_cols = w_key.shape[1]
    query_heads = query_cols // DH
    key_heads = key_cols // DH
    group_size = query_heads // key_heads
    gain_part = query_gain.shape[0]
    attn_cols = query_cols + 2 * key_cols

    owners = own_index ^ jnp.array(slot_offsets(ctx_count), jnp.int32)
    source_column = (owners[:, None] * shard_rows + jnp.arange(shard_rows)[None, :]).reshape(width)
    to_slots = (jnp.arange(width)[:, None] == source_column[None, :]).astype(jnp.bfloat16)
    states_slots = product(states, to_slots).astype(jnp.bfloat16)
    grad_out_slots = product(grad_out, to_slots).astype(jnp.bfloat16)

    packed_cols = attn_cols + query_cols
    small = jnp.concatenate(
        [attn_gain, ffn_gain, query_gain, key_gain, span_order[0].astype(jnp.bfloat16)]
    )
    small_rows = jnp.pad(small[None, :], ((0, EXTRA_ROWS - 1), (0, packed_cols - small.shape[0])))
    packed = jnp.concatenate(
        [jnp.concatenate([w_query, w_key, w_value, w_out.T], axis=1), small_rows], axis=0
    )
    packed_outer = gather_outer(packed, "ctx")
    gate_outer = gather_outer(after(w_gate, packed_outer), "ctx")
    up_first, up_first_arrived = gather_first(after(w_up, gate_outer), "ctx")
    packed_inner = gather_step(packed_outer, "ctx", 2)
    gathered = gather_step(packed_inner, "ctx", 1)
    gate_inner = gather_step(after(gate_outer, packed_inner), "ctx", 2)
    qkv_full = gathered[:, :shard_rows, :attn_cols].reshape(width, attn_cols)
    out_full = gathered[:, :shard_rows, attn_cols:].reshape(width, query_cols)
    small_full = gathered[:, shard_rows, : small.shape[0]]
    ends = [shard_rows, 2 * shard_rows, 2 * shard_rows + gain_part, 2 * shard_rows + 2 * gain_part]
    gain_attn = small_full[:, : ends[0]].reshape(width).astype(jnp.float32)
    gain_ffn = small_full[:, ends[0] : ends[1]].reshape(width).astype(jnp.float32)
    by_owner = (jnp.arange(ctx_count)[:, None] == owners[None, :]).astype(jnp.float32)
    gain_query = jnp.sum(
        by_owner[:, :, None] * small_full[None, :, ends[1] : ends[2]].astype(jnp.float32), axis=1
    ).reshape(DH)
    gain_key = jnp.sum(
        by_owner[:, :, None] * small_full[None, :, ends[2] : ends[3]].astype(jnp.float32), axis=1
    ).reshape(DH)
    order_slots = small_full[:, ends[3] :].astype(jnp.int32)
    offsets = jnp.arange(span_len, dtype=jnp.int32)
    every_place = (order_slots.reshape(ctx_count, sequences, 2, 1) * span_len + offsets).reshape(
        ctx_count, sequences, seq_rows
    )
    own_place = every_place[0]
    key_place = jnp.transpose(every_place, (1, 0, 2)).reshape(sequences, 1, ctx_count * seq_rows)
    query_place = jnp.tile(own_place, (1, group_size))[:, :, None]

    inputs = states_slots.astype(jnp.float32)
    normed_one, factor_one = norm_rows(inputs)
    hidden_one = (normed_one * gain_attn).astype(jnp.bfloat16)
    qkv = product(hidden_one, qkv_full)
    query_pre = qkv[:, :query_cols].reshape(token_rows, query_heads, DH)
    key_pre = qkv[:, query_cols : query_cols + key_cols].reshape(token_rows, key_heads, DH)
    value_low = qkv[:, query_cols + key_cols :].astype(jnp.bfloat16)
    half_dim = DH // 2
    inverse_freq = jnp.exp(-math.log(THETA) * jnp.arange(half_dim, dtype=jnp.float32) / half_dim)
    angles = own_place.reshape(token_rows).astype(jnp.float32)[:, None] * inverse_freq[None, :]
    cosine = jnp.cos(angles)[:, None, :]
    sine_part = jnp.sin(angles)[:, None, :]
    query_normed, query_factor = norm_rows(query_pre)
    key_normed, key_factor = norm_rows(key_pre)
    query_rot = rotate(query_normed * gain_query, cosine, sine_part).astype(jnp.bfloat16)
    key_rot = rotate(key_normed * gain_key, cosine, sine_part).astype(jnp.bfloat16)
    queries = to_heads(query_rot, sequences, key_heads, group_size)
    keys = to_heads(key_rot, sequences, key_heads, 1)
    values = to_heads(value_low, sequences, key_heads, 1)
    pairs_outer = gather_outer(
        after(jnp.concatenate([keys, values], axis=-1), up_first_arrived), "ctx"
    )
    up_outer = gather_rest(after(up_first, pairs_outer), up_first_arrived, "ctx")
    down_first, down_first_arrived = gather_first(after(w_down.T, up_outer), "ctx")
    pairs_inner = gather_step(after(pairs_outer, gate_inner), "ctx", 2)
    pairs = gather_step(pairs_inner, "ctx", 1)
    up_sent = after(up_outer, pairs_inner)
    up_arrived = swapped(up_sent, "ctx", 2)
    attend_inputs = (queries, pairs, query_place, key_place)
    (attended,) = attend_call(
        attend_kernel, attend_inputs, [jax.ShapeDtypeStruct(queries.shape, jnp.bfloat16)], 1
    )
    gate_full = gather_step(after(gate_inner, attended), "ctx", 1).reshape(width, -1)
    down_outer = gather_rest(down_first, after(down_first_arrived, attended), "ctx")
    down_sent = after(down_outer, up_arrived)
    down_arrived = swapped(down_sent, "ctx", 2)
    up_inner = jnp.concatenate([up_sent, after(up_arrived, attended)], axis=0)
    up_full = gather_step(up_inner, "ctx", 1).reshape(width, -1)
    mixed_low = from_heads(attended, group_size)
    attn_terms = jnp.einsum("ta,da->td", mixed_low, out_full, preferred_element_type=jnp.float32)
    middle = inputs + tp_sum(attn_terms.astype(jnp.bfloat16))
    normed_two, factor_two = norm_rows(middle)
    down_inner = jnp.concatenate([down_sent, after(down_arrived, normed_two)], axis=0)
    down_full = gather_step(down_inner, "ctx", 1).reshape(width, -1)
    hidden_two = (normed_two * gain_ffn).astype(jnp.bfloat16)
    gate_proj = product(hidden_two, gate_full)
    up_proj = product(hidden_two, up_full)
    sigmoid_gate = 1.0 / (1.0 + jnp.exp(-gate_proj))
    activated = gate_proj * sigmoid_gate
    inner = (activated * up_proj).astype(jnp.bfloat16)
    slotted = lambda grad: grad.astype(jnp.bfloat16).reshape(ctx_count, shard_rows, -1)
    down_grad = jnp.einsum("td,tf->df", grad_out_slots, inner, preferred_element_type=jnp.float32)
    down_kept, down_sent = halves_of(added(*scatter_step(slotted(down_grad), "ctx", 1)))
    down_arrived = swapped(down_sent, "ctx", 2)
    inner_grad = product(grad_out_slots, down_full)
    gate_grad = (
        inner_grad * up_proj * sigmoid_gate * (1.0 + gate_proj * (1.0 - sigmoid_gate))
    ).astype(jnp.bfloat16)
    up_grad = (inner_grad * activated).astype(jnp.bfloat16)
    hidden_two_part = jnp.einsum(
        "tf,cf->tc", after(gate_grad, down_sent), gate_full, preferred_element_type=jnp.float32
    ) + jnp.einsum("tf,cf->tc", up_grad, up_full, preferred_element_type=jnp.float32)
    hidden_two_grad = tp_sum(hidden_two_part.astype(jnp.bfloat16))
    gate_wgrad = jnp.einsum("tc,tf->cf", hidden_two, gate_grad, preferred_element_type=jnp.float32)
    gate_kept, gate_sent = halves_of(added(*scatter_step(slotted(gate_wgrad), "ctx", 1)))
    gate_arrived = swapped(after(gate_sent, down_arrived), "ctx", 2)
    up_wgrad = jnp.einsum("tc,tf->cf", hidden_two, up_grad, preferred_element_type=jnp.float32)
    up_core_kept, up_core_arrived = scatter_step(slotted(up_wgrad), "ctx", 1)
    ffn_gain_grad = jnp.sum(hidden_two_grad * normed_two, axis=0)
    middle_grad = grad_out_slots.astype(jnp.float32) + norm_back(
        hidden_two_grad, normed_two, factor_two, gain_ffn
    )
    branch_low = middle_grad.astype(jnp.bfloat16)
    out_wgrad = jnp.einsum("td,ta->da", branch_low, mixed_low, preferred_element_type=jnp.float32)
    mixed_grad = product(branch_low, out_full).astype(jnp.bfloat16)
    down_first = scatter_first(added(down_kept, after(down_arrived, middle_grad)), "ctx")
    attended_grad = to_heads(after(mixed_grad, gate_sent, down_arrived), sequences, key_heads, group_size)
    query_grad, pair_grad = attend_call(
        attend_back_kernel,
        attend_inputs + (attended_grad,),
        [
            jax.ShapeDtypeStruct(queries.shape, jnp.float32),
            jax.ShapeDtypeStruct(pairs.shape, jnp.bfloat16),
        ],
        3,
    )
    pair_core = scatter_step(after(pair_grad, gate_arrived, down_first[1]), "ctx", 1)
    pair_kept, pair_sent = halves_of(added(*pair_core))
    pair_arrived = swapped(pair_sent, "ctx", 2)
    pair_ready = after(pair_sent, pair_grad)
    down_last = scatter_last(down_first[0], after(down_first[1], pair_ready), "ctx")
    gate_first = scatter_first(added(gate_kept, after(gate_arrived, pair_ready)), "ctx")
    pair_first = scatter_first(
        after(added(pair_kept, pair_arrived), down_last[1], gate_first[1]), "ctx"
    )
    up_kept, up_sent = halves_of(added(up_core_kept, after(up_core_arrived, pair_arrived)))
    up_arrived = swapped(after(up_sent, gate_arrived), "ctx", 2)
    pair_last = scatter_last(*pair_first, "ctx")
    pair_share = total_of(*pair_last)
    gate_last = scatter_last(gate_first[0], after(gate_first[1], pair_last[1]), "ctx")
    down_share = total_of(*down_last)
    ffn_terms = jnp.einsum("tf,df->td", after(inner, pair_arrived), down_full, preferred_element_type=jnp.float32)
    output_slots = (middle + tp_sum(ffn_terms.astype(jnp.bfloat16))).astype(jnp.bfloat16)
    output_low = jnp.einsum(
        "td,ed->te", output_slots, to_slots, preferred_element_type=jnp.float32
    ).astype(jnp.bfloat16)
    query_rot_grad = from_heads(query_grad, group_size).reshape(token_rows, query_heads, DH)
    key_rot_grad = from_heads(pair_share[..., :DH], 1).reshape(token_rows, key_heads, DH)
    value_grad_low = from_heads(pair_share[..., DH:], 1).astype(jnp.bfloat16)
    query_out_grad = rotate(query_rot_grad, cosine, -sine_part)
    key_out_grad = rotate(key_rot_grad, cosine, -sine_part)
    query_gain_grad = jnp.sum(query_out_grad * query_normed, axis=(0, 1))
    key_gain_grad = jnp.sum(key_out_grad * key_normed, axis=(0, 1))
    query_pre_grad = norm_back(query_out_grad, query_normed, query_factor, gain_query)
    key_pre_grad = norm_back(key_out_grad, key_normed, key_factor, gain_key)
    qkv_grad = jnp.concatenate(
        [
            query_pre_grad.reshape(token_rows, query_cols).astype(jnp.bfloat16),
            key_pre_grad.reshape(token_rows, key_cols).astype(jnp.bfloat16),
            value_grad_low,
        ],
        axis=1,
    )
    qkv_grad = after(qkv_grad, up_arrived, gate_last[1])
    hidden_one_part = jnp.einsum(
        "ta,ca->tc", qkv_grad, qkv_full, preferred_element_type=jnp.float32
    )
    gain_terms = jnp.concatenate([query_gain_grad, key_gain_grad])[None, :]
    gain_rows = jnp.pad(gain_terms, ((0, EXTRA_ROWS - 1), (0, width - gain_terms.shape[1])))
    summed = tp_sum(jnp.concatenate([hidden_one_part, gain_rows], axis=0).astype(jnp.bfloat16))
    qkv_wgrad = jnp.einsum("tc,ta->ca", hidden_one, qkv_grad, preferred_element_type=jnp.float32)
    packed_core = scatter_step(
        slotted(jnp.concatenate([qkv_wgrad, out_wgrad], axis=1)), "ctx", 1
    )
    summed = after(summed, packed_core[1])
    hidden_one_grad = summed[:token_rows]
    attn_gain_grad = jnp.sum(hidden_one_grad * normed_one, axis=0)
    states_slots_grad = middle_grad + norm_back(
        hidden_one_grad, normed_one, factor_one, gain_attn
    )
    states_grad = jnp.einsum(
        "td,ed->te",
        states_slots_grad,
        to_slots.astype(jnp.float32),
        precision=lax.Precision.HIGHEST,
        preferred_element_type=jnp.float32,
    )
    gain_sums = summed[token_rows, : 2 * DH].reshape(2, ctx_count, gain_part)
    gain_slots = jnp.sum(by_owner[None, :, :, None] * gain_sums[:, :, None, :], axis=1)
    small_grads = jnp.concatenate(
        [
            attn_gain_grad.reshape(ctx_count, shard_rows),
            ffn_gain_grad.reshape(ctx_count, shard_rows),
            gain_slots[0],
            gain_slots[1],
        ],
        axis=1,
    ).astype(jnp.bfloat16)
    small_slots = added(*scatter_step(small_grads[:, None, :], "ctx", 1))
    small_slots = added(*scatter_step(small_slots, "ctx", 2))
    small_last = scatter_last(*scatter_first(small_slots, "ctx"), "ctx")
    small_share = total_of(*small_last)[0]
    packed_kept, packed_sent = halves_of(added(*packed_core))
    packed_arrived = swapped(packed_sent, "ctx", 2)
    up_first = scatter_first(added(up_kept, after(up_arrived, qkv_grad)), "ctx")
    up_last = scatter_last(*up_first, "ctx")
    packed_first = scatter_first(
        added(packed_kept, after(packed_arrived, up_last[1])), "ctx"
    )
    attn_share = total_of(*scatter_last(*packed_first, "ctx"))
    up_share = total_of(*up_last)
    gate_share = total_of(*gate_last)
    return (
        output_low,
        states_grad,
        small_share[: ends[0]],
        attn_share[:, :query_cols],
        attn_share[:, query_cols : query_cols + key_cols],
        attn_share[:, query_cols + key_cols : attn_cols],
        small_share[ends[1] : ends[2]],
        small_share[ends[2] : ends[3]],
        attn_share[:, attn_cols:].T,
        small_share[ends[0] : ends[1]],
        gate_share,
        up_share,
        down_share.T,
    )


def solution(mesh):
    in_specs = (
        P("ctx", None),
        P("ctx", None),
        P("ctx"),
        P("ctx", "tp"),
        P("ctx", "tp"),
        P("ctx", "tp"),
        P("ctx"),
        P("ctx"),
        P("tp", "ctx"),
        P("ctx"),
        P("ctx", "tp"),
        P("ctx", "tp"),
        P("tp", "ctx"),
        P("ctx", None),
    )
    out_specs = (
        P("ctx", None),
        P("ctx", None),
        P("ctx"),
        P("ctx", "tp"),
        P("ctx", "tp"),
        P("ctx", "tp"),
        P("ctx"),
        P("ctx"),
        P("tp", "ctx"),
        P("ctx"),
        P("ctx", "tp"),
        P("ctx", "tp"),
        P("tp", "ctx"),
    )
    return jax.shard_map(shards, mesh=mesh, in_specs=in_specs, out_specs=out_specs, check_vma=False)
```

```python
import math

import jax
import jax.numpy as jnp
from jax import lax
from jax.experimental import pallas as pl
from jax.experimental.pallas import tpu as pltpu
from jax.sharding import PartitionSpec as P

DH = 64


EPS = 1e-05
THETA = 1000000.0
SCALE = 0.125


VMEM_LIMIT = 48 * 1024 * 1024
EXTRA_ROWS = 16


def swapped(shard, axis, bit):
    devices = lax.axis_size(axis)
    return lax.ppermute(shard, axis, [(i, i ^ bit) for i in range(devices)])


def step_bits(devices):
    bits = []
    bit = devices // 2
    while bit:
        bits.append(bit)
        bit //= 2
    return bits


def slot_offsets(devices):
    offsets = [0]
    for bit in step_bits(devices):
        offsets = offsets + [item ^ bit for item in offsets]
    return offsets


def after(value, *earlier):
    return lax.optimization_barrier((value,) + earlier)[0]


def gather_step(gathered, axis, bit):
    return jnp.concatenate([gathered, swapped(gathered, axis, bit)], axis=0)


def gather_rest(sent, arrived, axis):
    gathered = jnp.concatenate([sent, arrived], axis=0)
    for bit in step_bits(lax.axis_size(axis))[1:-2]:
        gathered = gather_step(gathered, axis, bit)
    return gathered


def gather_first(shard, axis):
    return shard[None], swapped(shard[None], axis, lax.axis_size(axis) // 2)


def gather_outer(shard, axis):
    return gather_rest(*gather_first(shard, axis), axis)


def halves_of(slots):
    half = slots.shape[0] // 2
    return slots[:half], slots[half:]


def added(kept, arrived):
    return (kept.astype(jnp.float32) + arrived.astype(jnp.float32)).astype(jnp.bfloat16)


def scatter_step(slots, axis, bit):
    kept, sent = halves_of(slots)
    return kept, swapped(sent, axis, bit)


def scatter_first(slots, axis):
    return scatter_step(slots, axis, 4)


def scatter_last(kept, arrived, axis):
    for bit in reversed(step_bits(lax.axis_size(axis))[:-3]):
        kept, arrived = scatter_step(added(kept, arrived), axis, bit)
    return kept, arrived


def total_of(kept, arrived):
    return kept[0].astype(jnp.float32) + arrived[0].astype(jnp.float32)


def tp_sum(part):
    if lax.axis_size("tp") == 2:
        return part.astype(jnp.float32) + swapped(part, "tp", 1).astype(jnp.float32)
    return lax.psum(part, "tp").astype(jnp.float32)


def product(left, right):
    return jnp.dot(left, right, preferred_element_type=jnp.float32)


def norm_rows(values):
    factor = lax.rsqrt(jnp.mean(values * values, axis=-1, keepdims=True) + EPS)
    return (values * factor, factor)


def norm_back(gradient, normed, factor, gain):
    scaled = gradient * gain
    return factor * (scaled - normed * jnp.mean(scaled * normed, axis=-1, keepdims=True))


def rotate(values, cosine, sine_part):
    half_dim = values.shape[-1] // 2
    first_half = values[..., :half_dim]
    second_half = values[..., half_dim:]
    return jnp.concatenate(
        [
            first_half * cosine - second_half * sine_part,
            second_half * cosine + first_half * sine_part,
        ],
        axis=-1,
    )


def to_heads(flattened, sequences, key_heads, group_size):
    row_count = flattened.size // (sequences * key_heads * group_size * DH)
    arranged = flattened.reshape(sequences, row_count, key_heads, group_size, DH)
    return arranged.transpose(0, 2, 3, 1, 4).reshape(
        sequences, key_heads, group_size * row_count, DH
    )


def from_heads(stacked, group_size):
    sequences = stacked.shape[0]
    key_heads = stacked.shape[1]
    row_count = stacked.shape[2] // group_size
    arranged = stacked.reshape(sequences, key_heads, group_size, row_count, DH).transpose(
        0, 3, 1, 2, 4
    )
    return arranged.reshape(sequences * row_count, key_heads * group_size * DH)


def softmax_block(query_ref, pair_ref, query_place_ref, key_place_ref):
    pair = pair_ref[...]
    pair = pair.reshape(pair.shape[0] * pair.shape[3], pair.shape[4])
    key_rows = pair[:, :DH]
    value_rows = pair[:, DH:]
    query_rows = query_ref[0, 0] * SCALE
    scores = lax.dot_general(
        query_rows, key_rows, (((1,), (1,)), ((), ())), preferred_element_type=jnp.float32
    )
    scores = jnp.where(key_place_ref[0] <= query_place_ref[0], scores, -1e30)
    weights = jnp.exp(scores - jnp.max(scores, axis=-1, keepdims=True))
    weights = weights * (1.0 / jnp.sum(weights, axis=-1, keepdims=True))
    return query_rows, key_rows, value_rows, weights


def attend_kernel(query_ref, pair_ref, query_place_ref, key_place_ref, out_ref):
    unused_query, unused_key, value_rows, weights = softmax_block(
        query_ref, pair_ref, query_place_ref, key_place_ref
    )
    out_ref[0, 0] = product(weights.astype(jnp.bfloat16), value_rows).astype(out_ref.dtype)


def attend_back_kernel(
    query_ref, pair_ref, query_place_ref, key_place_ref, grad_ref, query_grad_ref, pair_grad_ref
):
    query_rows, key_rows, value_rows, weights = softmax_block(
        query_ref, pair_ref, query_place_ref, key_place_ref
    )
    grad_rows = grad_ref[0, 0]
    weight_grad = lax.dot_general(
        grad_rows, value_rows, (((1,), (1,)), ((), ())), preferred_element_type=jnp.float32
    )
    delta = jnp.sum(weights * weight_grad, axis=-1, keepdims=True)
    score_grad = (weights * (weight_grad - delta)).astype(jnp.bfloat16)
    query_grad_ref[0, 0] = product(score_grad, key_rows) * SCALE
    across = (((0,), (0,)), ((), ()))
    key_grad = lax.dot_general(
        score_grad, query_rows, across, preferred_element_type=jnp.float32
    )
    value_grad = lax.dot_general(
        weights.astype(jnp.bfloat16), grad_rows, across, preferred_element_type=jnp.float32
    )
    pair_grad = jnp.concatenate([key_grad, value_grad], axis=-1).astype(pair_grad_ref.dtype)
    pair_grad_ref[...] = pair_grad.reshape(pair_grad_ref.shape)


def attend_call(kernel, arrays, out_shapes, transcendentals):
    queries, pairs = arrays[0], arrays[1]
    sequences, key_heads, query_rows, unused = queries.shape
    slots, seq_rows = pairs.shape[0], pairs.shape[3]
    key_rows = slots * seq_rows

    def spec_of(array):
        if len(array.shape) == 5:
            return pl.BlockSpec((slots, 1, 1, seq_rows, 2 * DH), lambda s, h: (0, s, h, 0, 0))
        return pl.BlockSpec((1, 1, query_rows, DH), lambda s, h: (s, h, 0, 0))

    place_specs = [
        pl.BlockSpec((1, query_rows, 1), lambda s, h: (s, 0, 0)),
        pl.BlockSpec((1, 1, key_rows), lambda s, h: (s, 0, 0)),
    ]
    work = sequences * key_heads * query_rows * key_rows
    return pl.pallas_call(
        kernel,
        grid=(sequences, key_heads),
        in_specs=[spec_of(queries), spec_of(pairs)]
        + place_specs
        + [spec_of(array) for array in arrays[4:]],
        out_specs=[spec_of(shape) for shape in out_shapes],
        out_shape=out_shapes,
        compiler_params=pltpu.CompilerParams(vmem_limit_bytes=VMEM_LIMIT),
        cost_estimate=pl.CostEstimate(
            flops=4 * DH * work * transcendentals,
            bytes_accessed=4 * pairs.size,
            transcendentals=work,
        ),
    )(*arrays)


def shards(
    states,
    span_order,
    attn_gain,
    w_query,
    w_key,
    w_value,
    query_gain,
    key_gain,
    w_out,
    ffn_gain,
    w_gate,
    w_up,
    w_down,
    grad_out,
):
    ctx_count = lax.axis_size("ctx")
    own_index = lax.axis_index("ctx")
    token_rows, width = states.shape
    sequences = span_order.shape[1] // 2
    seq_rows = token_rows // sequences
    span_len = seq_rows // 2
    shard_rows = w_query.shape[0]
    query_cols = w_query.shape[1]
    key_cols = w_key.shape[1]
    query_heads = query_cols // DH
    key_heads = key_cols // DH
    group_size = query_heads // key_heads
    gain_part = query_gain.shape[0]
    attn_cols = query_cols + 2 * key_cols

    owners = own_index ^ jnp.array(slot_offsets(ctx_count), jnp.int32)
    source_column = (owners[:, None] * shard_rows + jnp.arange(shard_rows)[None, :]).reshape(width)
    to_slots = (jnp.arange(width)[:, None] == source_column[None, :]).astype(jnp.bfloat16)
    states_slots = product(states, to_slots).astype(jnp.bfloat16)
    grad_out_slots = product(grad_out, to_slots).astype(jnp.bfloat16)

    packed_cols = attn_cols + query_cols
    small = jnp.concatenate(
        [attn_gain, ffn_gain, query_gain, key_gain, span_order[0].astype(jnp.bfloat16)]
    )
    small_rows = jnp.pad(small[None, :], ((0, EXTRA_ROWS - 1), (0, packed_cols - small.shape[0])))
    packed = jnp.concatenate(
        [jnp.concatenate([w_query, w_key, w_value, w_out.T], axis=1), small_rows], axis=0
    )
    packed_outer = gather_outer(packed, "ctx")
    gate_outer = gather_outer(after(w_gate, packed_outer), "ctx")
    up_first, up_first_arrived = gather_first(after(w_up, gate_outer), "ctx")
    packed_inner = gather_step(packed_outer, "ctx", 2)
    gathered = gather_step(packed_inner, "ctx", 1)
    gate_inner = gather_step(after(gate_outer, packed_inner), "ctx", 2)
    qkv_full = gathered[:, :shard_rows, :attn_cols].reshape(width, attn_cols)
    out_full = gathered[:, :shard_rows, attn_cols:].reshape(width, query_cols)
    small_full = gathered[:, shard_rows, : small.shape[0]]
    ends = [shard_rows, 2 * shard_rows, 2 * shard_rows + gain_part, 2 * shard_rows + 2 * gain_part]
    gain_attn = small_full[:, : ends[0]].reshape(width).astype(jnp.float32)
    gain_ffn = small_full[:, ends[0] : ends[1]].reshape(width).astype(jnp.float32)
    by_owner = (jnp.arange(ctx_count)[:, None] == owners[None, :]).astype(jnp.float32)
    gain_query = jnp.sum(
        by_owner[:, :, None] * small_full[None, :, ends[1] : ends[2]].astype(jnp.float32), axis=1
    ).reshape(DH)
    gain_key = jnp.sum(
        by_owner[:, :, None] * small_full[None, :, ends[2] : ends[3]].astype(jnp.float32), axis=1
    ).reshape(DH)
    order_slots = small_full[:, ends[3] :].astype(jnp.int32)
    offsets = jnp.arange(span_len, dtype=jnp.int32)
    every_place = (order_slots.reshape(ctx_count, sequences, 2, 1) * span_len + offsets).reshape(
        ctx_count, sequences, seq_rows
    )
    own_place = every_place[0]
    key_place = jnp.transpose(every_place, (1, 0, 2)).reshape(sequences, 1, ctx_count * seq_rows)
    query_place = jnp.tile(own_place, (1, group_size))[:, :, None]

    inputs = states_slots.astype(jnp.float32)
    normed_one, factor_one = norm_rows(inputs)
    hidden_one = (normed_one * gain_attn).astype(jnp.bfloat16)
    qkv = product(hidden_one, qkv_full)
    query_pre = qkv[:, :query_cols].reshape(token_rows, query_heads, DH)
    key_pre = qkv[:, query_cols : query_cols + key_cols].reshape(token_rows, key_heads, DH)
    value_low = qkv[:, query_cols + key_cols :].astype(jnp.bfloat16)
    half_dim = DH // 2
    inverse_freq = jnp.exp(-math.log(THETA) * jnp.arange(half_dim, dtype=jnp.float32) / half_dim)
    angles = own_place.reshape(token_rows).astype(jnp.float32)[:, None] * inverse_freq[None, :]
    cosine = jnp.cos(angles)[:, None, :]
    sine_part = jnp.sin(angles)[:, None, :]
    query_normed, query_factor = norm_rows(query_pre)
    key_normed, key_factor = norm_rows(key_pre)
    query_rot = rotate(query_normed * gain_query, cosine, sine_part).astype(jnp.bfloat16)
    key_rot = rotate(key_normed * gain_key, cosine, sine_part).astype(jnp.bfloat16)
    queries = to_heads(query_rot, sequences, key_heads, group_size)
    keys = to_heads(key_rot, sequences, key_heads, 1)
    values = to_heads(value_low, sequences, key_heads, 1)
    pairs_outer = gather_outer(
        after(jnp.concatenate([keys, values], axis=-1), up_first_arrived), "ctx"
    )
    up_outer = gather_rest(after(up_first, pairs_outer), up_first_arrived, "ctx")
    down_first, down_first_arrived = gather_first(after(w_down.T, up_outer), "ctx")
    pairs_inner = gather_step(after(pairs_outer, gate_inner), "ctx", 2)
    pairs = gather_step(pairs_inner, "ctx", 1)
    up_sent = after(up_outer, pairs_inner)
    up_arrived = swapped(up_sent, "ctx", 2)
    attend_inputs = (queries, pairs, query_place, key_place)
    (attended,) = attend_call(
        attend_kernel, attend_inputs, [jax.ShapeDtypeStruct(queries.shape, jnp.bfloat16)], 1
    )
    gate_full = gather_step(after(gate_inner, attended), "ctx", 1).reshape(width, -1)
    down_outer = gather_rest(down_first, after(down_first_arrived, attended), "ctx")
    down_sent = after(down_outer, up_arrived)
    down_arrived = swapped(down_sent, "ctx", 2)
    up_inner = jnp.concatenate([up_sent, after(up_arrived, attended)], axis=0)
    up_full = gather_step(up_inner, "ctx", 1).reshape(width, -1)
    mixed_low = from_heads(attended, group_size)
    attn_terms = jnp.einsum("ta,da->td", mixed_low, out_full, preferred_element_type=jnp.float32)
    middle = inputs + tp_sum(attn_terms.astype(jnp.bfloat16))
    normed_two, factor_two = norm_rows(middle)
    down_inner = jnp.concatenate([down_sent, after(down_arrived, normed_two)], axis=0)
    down_full = gather_step(down_inner, "ctx", 1).reshape(width, -1)
    hidden_two = (normed_two * gain_ffn).astype(jnp.bfloat16)
    gate_proj = product(hidden_two, gate_full)
    up_proj = product(hidden_two, up_full)
    sigmoid_gate = 1.0 / (1.0 + jnp.exp(-gate_proj))
    activated = gate_proj * sigmoid_gate
    inner = (activated * up_proj).astype(jnp.bfloat16)
    slotted = lambda grad: grad.astype(jnp.bfloat16).reshape(ctx_count, shard_rows, -1)
    down_grad = jnp.einsum("td,tf->df", grad_out_slots, inner, preferred_element_type=jnp.float32)
    down_kept, down_sent = halves_of(added(*scatter_step(slotted(down_grad), "ctx", 1)))
    down_arrived = swapped(down_sent, "ctx", 2)
    inner_grad = product(grad_out_slots, down_full)
    gate_grad = (
        inner_grad * up_proj * sigmoid_gate * (1.0 + gate_proj * (1.0 - sigmoid_gate))
    ).astype(jnp.bfloat16)
    up_grad = (inner_grad * activated).astype(jnp.bfloat16)
    hidden_two_part = jnp.einsum(
        "tf,cf->tc", after(gate_grad, down_sent), gate_full, preferred_element_type=jnp.float32
    ) + jnp.einsum("tf,cf->tc", up_grad, up_full, preferred_element_type=jnp.float32)
    hidden_two_grad = tp_sum(hidden_two_part.astype(jnp.bfloat16))
    gate_wgrad = jnp.einsum("tc,tf->cf", hidden_two, gate_grad, preferred_element_type=jnp.float32)
    gate_kept, gate_sent = halves_of(added(*scatter_step(slotted(gate_wgrad), "ctx", 1)))
    gate_arrived = swapped(after(gate_sent, down_arrived), "ctx", 2)
    up_wgrad = jnp.einsum("tc,tf->cf", hidden_two, up_grad, preferred_element_type=jnp.float32)
    up_core_kept, up_core_arrived = scatter_step(slotted(up_wgrad), "ctx", 1)
    ffn_gain_grad = jnp.sum(hidden_two_grad * normed_two, axis=0)
    middle_grad = grad_out_slots.astype(jnp.float32) + norm_back(
        hidden_two_grad, normed_two, factor_two, gain_ffn
    )
    branch_low = middle_grad.astype(jnp.bfloat16)
    out_wgrad = jnp.einsum("td,ta->da", branch_low, mixed_low, preferred_element_type=jnp.float32)
    mixed_grad = product(branch_low, out_full).astype(jnp.bfloat16)
    down_first = scatter_first(added(down_kept, after(down_arrived, middle_grad)), "ctx")
    attended_grad = to_heads(after(mixed_grad, gate_sent, down_arrived), sequences, key_heads, group_size)
    query_grad, pair_grad = attend_call(
        attend_back_kernel,
        attend_inputs + (attended_grad,),
        [
            jax.ShapeDtypeStruct(queries.shape, jnp.float32),
            jax.ShapeDtypeStruct(pairs.shape, jnp.bfloat16),
        ],
        3,
    )
    pair_core = scatter_step(after(pair_grad, gate_arrived, down_first[1]), "ctx", 1)
    pair_kept, pair_sent = halves_of(added(*pair_core))
    pair_arrived = swapped(pair_sent, "ctx", 2)
    pair_ready = after(pair_sent, pair_grad)
    down_last = scatter_last(down_first[0], after(down_first[1], pair_ready), "ctx")
    gate_first = scatter_first(added(gate_kept, after(gate_arrived, pair_ready)), "ctx")
    pair_first = scatter_first(
        after(added(pair_kept, pair_arrived), down_last[1], gate_first[1]), "ctx"
    )
    up_kept, up_sent = halves_of(added(up_core_kept, after(up_core_arrived, pair_arrived)))
    up_arrived = swapped(after(up_sent, gate_arrived), "ctx", 2)
    pair_last = scatter_last(*pair_first, "ctx")
    pair_share = total_of(*pair_last)
    gate_last = scatter_last(gate_first[0], after(gate_first[1], pair_last[1]), "ctx")
    down_share = total_of(*down_last)
    ffn_terms = jnp.einsum("tf,df->td", after(inner, pair_arrived), down_full, preferred_element_type=jnp.float32)
    output_slots = (middle + tp_sum(ffn_terms.astype(jnp.bfloat16))).astype(jnp.bfloat16)
    output_low = jnp.einsum(
        "td,ed->te", output_slots, to_slots, preferred_element_type=jnp.float32
    ).astype(jnp.bfloat16)
    query_rot_grad = from_heads(query_grad, group_size).reshape(token_rows, query_heads, DH)
    key_rot_grad = from_heads(pair_share[..., :DH], 1).reshape(token_rows, key_heads, DH)
    value_grad_low = from_heads(pair_share[..., DH:], 1).astype(jnp.bfloat16)
    query_out_grad = rotate(query_rot_grad, cosine, -sine_part)
    key_out_grad = rotate(key_rot_grad, cosine, -sine_part)
    query_gain_grad = jnp.sum(query_out_grad * query_normed, axis=(0, 1))
    key_gain_grad = jnp.sum(key_out_grad * key_normed, axis=(0, 1))
    query_pre_grad = norm_back(query_out_grad, query_normed, query_factor, gain_query)
    key_pre_grad = norm_back(key_out_grad, key_normed, key_factor, gain_key)
    qkv_grad = jnp.concatenate(
        [
            query_pre_grad.reshape(token_rows, query_cols).astype(jnp.bfloat16),
            key_pre_grad.reshape(token_rows, key_cols).astype(jnp.bfloat16),
            value_grad_low,
        ],
        axis=1,
    )
    qkv_grad = after(qkv_grad, up_arrived)
    hidden_one_part = jnp.einsum(
        "ta,ca->tc", qkv_grad, qkv_full, preferred_element_type=jnp.float32
    )
    gain_terms = jnp.concatenate([query_gain_grad, key_gain_grad])[None, :]
    gain_rows = jnp.pad(gain_terms, ((0, EXTRA_ROWS - 1), (0, width - gain_terms.shape[1])))
    summed = tp_sum(jnp.concatenate([hidden_one_part, gain_rows], axis=0).astype(jnp.bfloat16))
    qkv_wgrad = jnp.einsum("tc,ta->ca", hidden_one, qkv_grad, preferred_element_type=jnp.float32)
    packed_core = scatter_step(
        slotted(jnp.concatenate([qkv_wgrad, out_wgrad], axis=1)), "ctx", 1
    )
    summed = after(summed, packed_core[1])
    hidden_one_grad = summed[:token_rows]
    attn_gain_grad = jnp.sum(hidden_one_grad * normed_one, axis=0)
    states_slots_grad = middle_grad + norm_back(
        hidden_one_grad, normed_one, factor_one, gain_attn
    )
    states_grad = jnp.einsum(
        "td,ed->te",
        states_slots_grad,
        to_slots.astype(jnp.float32),
        precision=lax.Precision.HIGHEST,
        preferred_element_type=jnp.float32,
    )
    gain_sums = summed[token_rows, : 2 * DH].reshape(2, ctx_count, gain_part)
    gain_slots = jnp.sum(by_owner[None, :, :, None] * gain_sums[:, :, None, :], axis=1)
    small_grads = jnp.concatenate(
        [
            attn_gain_grad.reshape(ctx_count, shard_rows),
            ffn_gain_grad.reshape(ctx_count, shard_rows),
            gain_slots[0],
            gain_slots[1],
        ],
        axis=1,
    ).astype(jnp.bfloat16)
    small_slots = added(*scatter_step(small_grads[:, None, :], "ctx", 1))
    small_slots = added(*scatter_step(small_slots, "ctx", 2))
    small_last = scatter_last(*scatter_first(small_slots, "ctx"), "ctx")
    small_share = total_of(*small_last)[0]
    packed_kept, packed_sent = halves_of(added(*packed_core))
    packed_arrived = swapped(packed_sent, "ctx", 2)
    up_first = scatter_first(
        added(up_kept, after(up_arrived, packed_core[1], gate_last[1])), "ctx"
    )
    up_last = scatter_last(*up_first, "ctx")
    packed_first = scatter_first(
        added(packed_kept, after(packed_arrived, up_last[1])), "ctx"
    )
    attn_share = total_of(*scatter_last(*packed_first, "ctx"))
    up_share = total_of(*up_last)
    gate_share = total_of(*gate_last)
    return (
        output_low,
        states_grad,
        small_share[: ends[0]],
        attn_share[:, :query_cols],
        attn_share[:, query_cols : query_cols + key_cols],
        attn_share[:, query_cols + key_cols : attn_cols],
        small_share[ends[1] : ends[2]],
        small_share[ends[2] : ends[3]],
        attn_share[:, attn_cols:].T,
        small_share[ends[0] : ends[1]],
        gate_share,
        up_share,
        down_share.T,
    )


def solution(mesh):
    in_specs = (
        P("ctx", None),
        P("ctx", None),
        P("ctx"),
        P("ctx", "tp"),
        P("ctx", "tp"),
        P("ctx", "tp"),
        P("ctx"),
        P("ctx"),
        P("tp", "ctx"),
        P("ctx"),
        P("ctx", "tp"),
        P("ctx", "tp"),
        P("tp", "ctx"),
        P("ctx", None),
    )
    out_specs = (
        P("ctx", None),
        P("ctx", None),
        P("ctx"),
        P("ctx", "tp"),
        P("ctx", "tp"),
        P("ctx", "tp"),
        P("ctx"),
        P("ctx"),
        P("tp", "ctx"),
        P("ctx"),
        P("ctx", "tp"),
        P("ctx", "tp"),
        P("tp", "ctx"),
    )
    return jax.shard_map(shards, mesh=mesh, in_specs=in_specs, out_specs=out_specs, check_vma=False)
```
